512 devices in a mesh: blk: 64 (over y, x, core), tp: 8 (over z).
Axes of the slice: x: 4, y: 8, z: 8, core: 2. Of those that a mesh axis runs over, the one named last changes fastest.
Arguments:
- inputs: bfloat16 [8192, 8192], P('blk', 'tp'), may hold values from -6 to 6
- grad_out: bfloat16 [8192, 8192], P('blk', 'tp'), may hold values from -6 to 6
- w_up: bfloat16 [128, 2, 128, 128], P('blk'), may hold values from -0.4375 to 0.4375
- w_down: bfloat16 [128, 2, 128, 128], P('blk'), may hold values from -0.3125 to 0.3125
- up_rows: int32 [128, 2], P('blk'), may hold values from 0 to 63, as said below
- slot_counts: int32 [128], P('blk'), may hold values from 1 to 2
- keep_mask: int32 [8192, 1024], P(None, 'blk'), may hold values from 0 to 65535, as said below
Outputs:
- outputs: bfloat16 [8192, 8192], P('blk', 'tp')
- grad_in: bfloat16 [8192, 8192], P('blk', 'tp')
- grad_up: bfloat16 [128, 2, 128, 128], P('blk', None, 'tp')
- grad_down: bfloat16 [128, 2, 128, 128], P('blk', None, 'tp')
The draws below stay inside these ranges and needn't reach their ends.
Inputs may be any that keep to these rules, and one draw needn't show every extreme that they name: `up_rows`: within each hidden column block, the 2 entries are distinct. `keep_mask`: bit k of word w holds the keep flag of hidden unit 16 w + k.
All inputs are finite; a program needn't handle non-finite values.
Results may differ from the reference program's by a relative error of at most 0.005.
Values may be sent and summed in bfloat16 or wider, within the bound.
A program may use at most 64 MiB of HBM per device.

```python
import jax
import jax.numpy as jnp
from jax import lax

D = 8192
TILE = 128
SLOTS = 2
TOKENS = 8192
COL_BLOCKS = 128
FF = 16384


def draw_up_rows(key, part):
    row_total = D // TILE
    scores = jax.random.randint(key, (COL_BLOCKS, row_total), 0, 1 << 20)
    scores = scores * row_total + jnp.arange(row_total, dtype=jnp.int32)
    order = jnp.argsort(scores, axis=-1)
    return order[:, :SLOTS].astype(jnp.int32)


def draw_keep_mask(key, part):
    flags = (jax.random.randint(key, (TOKENS, FF // 16, 16), 0, 5) > 0).astype(jnp.int32)
    powers = jnp.left_shift(jnp.ones((16,), jnp.int32), jnp.arange(16, dtype=jnp.int32))
    return jnp.sum(flags * powers, axis=-1).astype(jnp.int32)


def touch_ends(entries, own_key, smallest, high):
    longest = entries.shape.index(max(entries.shape))
    spots = []
    for shift in (0, 1):
        where = [jax.random.randint(jax.random.fold_in(own_key, axis), (), 0, length) for axis, length in enumerate(entries.shape)]
        where[longest] = (where[longest] + shift) % entries.shape[longest]
        spots.append(tuple(where))
    return entries.at[spots[0]].set(smallest).at[spots[1]].set(high)


def block_scale(key, extent, cuts, smallest, top_value):
    factor_of = 1.0
    for position, shards_of in cuts:
        draws = jax.random.uniform(jax.random.fold_in(jax.random.fold_in(key, 6), position), (shards_of,), jnp.float32, smallest / len(cuts), top_value / len(cuts))
        factor_of = factor_of * jnp.repeat(jnp.exp(draws), extent[position] // shards_of).reshape((-1,) + (1,) * (len(extent) - 1 - position))
    return factor_of


def gaussian(own_key, extent, scale, limit, pieces=(), kind=jnp.bfloat16):
    drawn = scale * jax.random.normal(own_key, extent, jnp.float32)
    if pieces:
        drawn = drawn * block_scale(own_key, extent, pieces, -0.22, 0.18)
    return jnp.clip(drawn, -limit, limit).astype(kind)


def setup_inputs(seed: int = 0) -> dict:
    keys = jax.random.split(jax.random.key(seed), 8)
    return {
        "inputs": gaussian(keys[0], (TOKENS, D), 1.0, 6.0, ((0, 64), (1, 8))),
        "grad_out": gaussian(keys[1], (TOKENS, D), 1.0, 6.0, ((0, 64), (1, 8))),
        "w_up": gaussian(keys[2], (COL_BLOCKS, SLOTS, TILE, TILE), ((SLOTS + 1) * TILE // 2) ** -0.5, 0.4375, ((0, 64),)),
        "w_down": gaussian(keys[3], (COL_BLOCKS, SLOTS, TILE, TILE), (COL_BLOCKS * (SLOTS + 1) * TILE // (2 * (D // TILE))) ** -0.5, 0.3125, ((0, 64),)),
        "up_rows": draw_up_rows(jax.random.fold_in(keys[7], 71), 0),
        "slot_counts": touch_ends(jax.random.randint(keys[5], (COL_BLOCKS,), 1, SLOTS + 1), jax.random.fold_in(keys[5], 1), 1, SLOTS).astype(jnp.int32),
        "keep_mask": draw_keep_mask(jax.random.fold_in(keys[7], 71), 0),
    }


INV_ROOT_TWO = 0.7071067811865476
INV_ROOT_TAU = 0.3989422804014327
KEEP_SCALE = 1.25


def gelu_value(value):
    return 0.5 * value * (1.0 + jax.scipy.special.erf(value * INV_ROOT_TWO))


def gelu_slope(value):
    return 0.5 * (1.0 + jax.scipy.special.erf(value * INV_ROOT_TWO)) + value * jnp.exp(-0.5 * value * value) * INV_ROOT_TAU


def reference(inputs, grad_out, w_up, w_down, up_rows, slot_counts, keep_mask):
    row_total = D // TILE
    slot_index = jnp.arange(SLOTS, dtype=jnp.int32)
    column = jnp.arange(TILE, dtype=jnp.int32)
    input_blocks = inputs.reshape(TOKENS, row_total, TILE)
    cotangent_blocks = grad_out.reshape(TOKENS, row_total, TILE)
    block_ids = jnp.arange(COL_BLOCKS, dtype=jnp.int32)

    def one_block(carry, items):
        out_acc, grad_acc = carry
        up_tiles, down_tiles, rows, count, block = items
        rows = rows.astype(jnp.int32)
        live = (slot_index < count).astype(jnp.float32)
        up_live = up_tiles.astype(jnp.float32) * live[:, None, None]
        down_live = down_tiles.astype(jnp.float32) * live[:, None, None]
        hidden_cols = (block * TILE + column).astype(jnp.int32)
        words = jnp.take(keep_mask, hidden_cols // 16, axis=1)
        keep = jnp.bitwise_and(jnp.right_shift(words, hidden_cols % 16), 1)
        scale = keep.astype(jnp.float32) * KEEP_SCALE
        input_tiles = jnp.take(input_blocks, rows, axis=1).astype(jnp.float32)
        cotangent_tiles = jnp.take(cotangent_blocks, rows, axis=1).astype(jnp.float32)
        pre = jnp.einsum("nsi,sij->nj", input_tiles, up_live)
        hidden = (gelu_value(pre) * scale).astype(jnp.bfloat16)
        hidden_wide = hidden.astype(jnp.float32)
        out_terms = jnp.einsum("nj,sjk->nsk", hidden_wide, down_live)
        out_acc = out_acc.at[:, rows, :].add(out_terms)
        grad_hidden = jnp.einsum("nsk,sjk->nj", cotangent_tiles, down_live)
        grad_pre = (grad_hidden * scale * gelu_slope(pre)).astype(jnp.bfloat16)
        grad_wide = grad_pre.astype(jnp.float32)
        grad_terms = jnp.einsum("nj,sij->nsi", grad_wide, up_live)
        grad_acc = grad_acc.at[:, rows, :].add(grad_terms)
        up_grad = (jnp.einsum("nsi,nj->sij", input_tiles, grad_wide) * live[:, None, None]).astype(jnp.bfloat16)
        down_grad = (jnp.einsum("nj,nsk->sjk", hidden_wide, cotangent_tiles) * live[:, None, None]).astype(jnp.bfloat16)
        return (out_acc, grad_acc), (up_grad, down_grad)

    start = (jnp.zeros((TOKENS, row_total, TILE), jnp.float32), jnp.zeros((TOKENS, row_total, TILE), jnp.float32))
    (out_acc, grad_acc), (grad_up, grad_down) = lax.scan(one_block, start, (w_up, w_down, up_rows, slot_counts, block_ids))
    outputs = out_acc.reshape(TOKENS, D).astype(jnp.bfloat16)
    grad_in = grad_acc.reshape(TOKENS, D).astype(jnp.bfloat16)
    return (outputs, grad_in, grad_up, grad_down)
```

```python
import functools

import jax
import jax.numpy as jnp
from jax import lax
from jax.experimental import pallas as pl
from jax.experimental.pallas import tpu as pltpu
from jax.sharding import PartitionSpec as P

INV_ROOT_TWO = 0.7071067811865476
INV_ROOT_TAU = 0.3989422804014327
KEEP_SCALE = 1.25
MESH = pl.DeviceIdType.MESH
X_CHIPS = 4
BF = jnp.bfloat16
F32 = jnp.float32
I32 = jnp.int32


def dot(a, b, ca, cb):
    return lax.dot_general(a, b, (((ca,), (cb,)), ((), ())), preferred_element_type=F32)


def iota(shape, dim):
    return lax.broadcasted_iota(I32, shape, dim)


def kernel(
    dims,
    x_ref, dy_ref, wu_ref, wd_ref, keep_ref, rows_ref, cnt_ref,
    out_ref, gin_ref, gup_ref, gdn_ref,
    zst, full_x, full_dy, rows_a, rows_b, rows_s, wu, wd, tokw, maskw, mask_st, scale,
    tile_st, tile_in, slope, hid, gpre, term_st, term_in, lanes, hot,
    zo_st, zo_in, gst, gin_z, gsum, gpart,
    z_send, z_recv, a_send, a_recv, b_send, b_recv, p_send, p_recv,
    d_send, d_recv, t_send, t_recv, o_send, o_recv, g_send, g_recv, l_sem,
):
    YN, XN, ZN, PT, RL = dims
    XC = XN * 2
    HALF = YN // 2
    LO = HALF // 2 - 1
    ND = HALF * XC
    RB = RL * ZN
    GT = XC * PT
    blk, z = lax.axis_index("blk"), lax.axis_index("tp")
    c = lax.rem(blk, 2)
    x = lax.rem(blk // 2, XN)
    y = blk // XC
    xc = x * 2 + c
    up = jnp.where(y >= HALF, 1, 0)
    partner = lax.rem(y + HALF, YN) * XC + xc

    def mod(v, n):
        return lax.rem(v + n, n)

    def remote(src, dst, ss, rs, b, t):
        return pltpu.make_async_remote_copy(
            src_ref=src, dst_ref=dst, send_sem=ss, recv_sem=rs, device_id=(b, t), device_id_type=MESH
        )

    barrier = pltpu.get_barrier_semaphore()
    peers = []
    for dy in range(-(HALF // 2), YN - HALF // 2):
        for xo in range(XN):
            for co in range(2):
                if (dy, xo, co) == (0, 0, 0):
                    continue
                if abs(dy) <= HALF // 2 or (xo, co) == (0, 0):
                    peers.append((mod(y + dy, YN) * XC + lax.rem(x + xo, XN) * 2 + lax.rem(c + co, 2), z))
    for zo in range(1, ZN):
        peers.append((blk, lax.rem(z + zo, ZN)))
    for b, t in peers:
        pl.semaphore_signal(barrier, inc=1, device_id=(b, t), device_id_type=MESH)

    full = (full_x, full_dy)
    lane = iota((8, 128), 1)
    mine = jnp.where(lane == 0, rows_ref[0, 0], jnp.where(lane == 1, rows_ref[0, 1],
                     jnp.where(lane == 2, rows_ref[1, 0], rows_ref[1, 1])))
    rows_a[xc] = mine
    for a, ref in enumerate((x_ref, dy_ref)):
        for t in range(ZN):
            for i in range(RL):
                zst[a, t, i] = ref[t * PT:(t + 1) * PT, i * 128:(i + 1) * 128]
        full[a][pl.ds(z * RL, RL)] = zst[a, z]
    for cl in range(2):
        for s in range(2):
            live = s < cnt_ref[cl]
            wu[2 * up + cl, s * 128:(s + 1) * 128, :] = jnp.where(live, wu_ref[cl, s], jnp.zeros((), BF))
            wd[2 * up + cl, :, s * 128:(s + 1) * 128] = jnp.where(live, wd_ref[cl, s], jnp.zeros((), BF))
    pl.semaphore_wait(barrier, len(peers))

    def row_a(o):
        q = lax.rem(xc + o, XC)
        return remote(rows_a.at[xc], rows_a.at[xc], a_send.at[o], a_recv.at[xc], y * XC + q, z)

    for o in range(1, XC):
        row_a(o).start()

    order = [o for k in range(1, ZN // 2 + 1) for o in dict.fromkeys((k, ZN - k))]

    def z_copy(a, o):
        t = lax.rem(z + o, ZN)
        return remote(zst.at[a, t], full[a].at[pl.ds(z * RL, RL)], z_send.at[a, o], z_recv.at[a, z], blk, t)

    for a in range(2):
        for o in order:
            z_copy(a, o).start()
    w_copies = [
        remote(w.at[pl.ds(2 * up, 2)], w.at[pl.ds(2 * up, 2)], p_send.at[k], p_recv.at[k], partner, z)
        for k, w in enumerate((wu, wd))
    ]
    for w_copy in w_copies:
        w_copy.start()

    span = XC * ZN * PT
    r, l = iota((span, GT), 0), iota((span, GT), 1)
    share = ZN * PT
    pick = jnp.where((r // share == l // PT) & (lax.rem(r, share) == z * PT + lax.rem(l, PT)), 1.0, 0.0).astype(BF)
    for g in range(YN):
        words = keep_ref[:, g * span:(g + 1) * span]
        low = jnp.bitwise_and(words, 255).astype(F32).astype(BF)
        high = jnp.right_shift(words, 8).astype(F32).astype(BF)
        found = dot(jnp.concatenate([low, high], axis=0), pick, 1, 0).astype(I32)
        tokw[g] = found[:16] + found[16:] * 256
    for j in range(HALF):
        maskw[up, j] = tokw[mod(y + j - LO - c, YN)]
        mask_st[j] = tokw[lax.rem(y + HALF + j - LO - c + YN, YN)]
    m_copy = remote(mask_st, maskw.at[up], p_send.at[2], p_recv.at[2], partner, z)
    m_copy.start()

    def wait_a(o):
        q = lax.rem(xc + o, XC)
        remote(rows_a.at[q], rows_a.at[q], a_send.at[o], a_recv.at[q], blk, z).wait_recv()

    for o in range(1, XC):
        wait_a(o)
    sub = iota((8, 128), 0)
    packed = rows_a[0]
    for q in range(1, XC):
        packed = jnp.where(sub == q, rows_a[q], packed)
    rows_b[y] = packed

    def row_b(o):
        q = lax.rem(y + o, YN)
        return remote(rows_b.at[y], rows_b.at[y], b_send.at[o], b_recv.at[y], q * XC + xc, z)

    for o in range(1, YN):
        row_b(o).start()
    for o in range(1, YN):
        q = lax.rem(y + o, YN)
        remote(rows_b.at[q], rows_b.at[q], b_send.at[o], b_recv.at[q], blk, z).wait_recv()
    to_scalar = pltpu.make_async_copy(rows_b, rows_s, l_sem)
    to_scalar.start()
    to_scalar.wait()

    def label(i):
        j = lax.rem(i, HALF)
        xo = lax.rem(i // HALF, XN)
        co = i // (HALF * XN)
        xd, cd = lax.rem(x + xo, XN), lax.rem(c + co, 2)
        return j, xd, cd, j * XC + xd * 2 + cd

    def token_side(i):
        j, xd, cd, d = label(i)
        yd = lax.rem(y - (j - LO - cd) + YN, YN)
        return d, yd, xd, cd, (yd == y) & (xd == x) & (cd == c), j * XC + xc

    def owner_side(i):
        j, xd, cd, d = label(i)
        yd = lax.rem(y + (j - LO - c) + YN, YN)
        return d, yd, xd, cd, (yd == y) & (xd == x) & (cd == c), j * XC + xc

    def tile_copy(a, i):
        d, yd, xd, cd, own, at = token_side(i)
        return own, lambda: remote(
            tile_st.at[a, d], tile_in.at[a, at], d_send.at[a, d], d_recv.at[a, at], yd * XC + xd * 2 + cd, z
        ), lambda: pltpu.make_async_copy(tile_st.at[a, d], tile_in.at[a, at], d_recv.at[a, at])

    def dispatch(a):
        for o in order:
            s = lax.rem(z + o, ZN)
            remote(zst.at[a, s], full[a].at[pl.ds(s * RL, RL)], z_send.at[a, o], z_recv.at[a, s], blk, z).wait_recv()

        @pl.loop(0, ND)
        def _(i):
            d, yd, xd, cd, own, at = token_side(i)
            low = lax.rem(yd, HALF)
            for k in range(8):
                row = rows_s[low + HALF * (k // 4), xd * 2 + cd, k % 4]
                tile_st[a, d, k] = full[a][row]
            own, far, near = tile_copy(a, i)

            @pl.when(own)
            def _():
                near().start()

            @pl.when(jnp.logical_not(own))
            def _():
                far().start()

    dispatch(0)
    dispatch(1)

    @pl.loop(0, ND)
    def _(i):
        d, yd, xd, cd, own, at = token_side(i)
        low = lax.rem(yd, HALF)
        value = jnp.zeros((8, 128), I32)
        for k in range(8):
            row = rows_s[low + HALF * (k // 4), xd * 2 + cd, k % 4]
            value = jnp.where(lane // PT == k, row * PT, value)
        lanes[d] = value + lax.rem(lane, PT)

    @pl.loop(0, ND)
    def _(d):
        want = lanes[d][0:1, :]
        at = pl.ds(pl.multiple_of(d * 128, 128), 128)
        hot[:, at] = jnp.where(iota((RB * PT, 128), 0) == want, 1.0, 0.0).astype(BF)

    m_wait = remote(mask_st, maskw.at[1 - up], p_send.at[2], p_recv.at[2], partner, z)
    m_wait.wait_recv()
    er, el = iota((32, 256), 0), iota((32, 256), 1)
    spread = jnp.where((el // 16 == lax.rem(er, 16)) & ((lax.rem(el, 16) >= 8) == (er >= 16)), 1.0, 0.0).astype(BF)
    shift = lax.rem(iota((GT, 256), 1), 8)
    for h in range(2):
        for j in range(HALF):
            words = maskw[h, j]
            low = jnp.bitwise_and(words, 255).astype(F32).astype(BF)
            high = jnp.right_shift(words, 8).astype(F32).astype(BF)
            found = dot(jnp.concatenate([low, high], axis=0), spread, 0, 0).astype(I32)
            keep = jnp.bitwise_and(jnp.right_shift(found, shift), 1)
            scale[h, j * GT:(j + 1) * GT, :] = keep.astype(F32) * KEEP_SCALE
    for k, w in enumerate((wu, wd)):
        there = w.at[pl.ds(2 * (1 - up), 2)]
        remote(there, there, p_send.at[k], p_recv.at[k], partner, z).wait_recv()

    def wide(a, col, start, count):
        parts = [tile_in[a, pl.ds(start, count), 2 * col + s].reshape(count * PT, 128) for s in range(2)]
        return jnp.concatenate(parts, axis=1)

    def term_copy(a, i):
        d, yd, xd, cd, own, at = owner_side(i)
        return own, lambda: remote(
            term_st.at[a, d], term_in.at[a, at], t_send.at[a, d], t_recv.at[a, at], yd * XC + xd * 2 + cd, z
        ), lambda: pltpu.make_async_copy(term_st.at[a, d], term_in.at[a, at], t_recv.at[a, at])

    def wait_slot(buf, sem, a, d):
        remote(buf.at[a, d], buf.at[a, d], sem.at[a, d], sem.at[a, d], blk, z).wait_recv()

    def put(a, col, g, value):
        value = value.astype(BF)
        for s in range(2):
            term_st[a, pl.ds(g * XC, XC), 2 * col + s] = value[:, s * 128:(s + 1) * 128].reshape(XC, PT, 128)

    def send_group(a, g):
        @pl.loop(0, XC)
        def _(q):
            own, far, near = term_copy(a, q * HALF + g)

            @pl.when(own)
            def _():
                near().start()

            @pl.when(jnp.logical_not(own))
            def _():
                far().start()

    @pl.loop(0, HALF)
    def _(g):
        @pl.loop(0, XC)
        def _(q):
            wait_slot(tile_in, d_recv, 0, g * XC + q)

        toks = pl.ds(pl.multiple_of(g * GT, GT), GT)
        for col in range(4):
            pre = dot(wide(0, col, g * XC, XC), wu[col], 1, 0)
            part = 0.5 * (1.0 + lax.erf(pre * INV_ROOT_TWO))
            keep = scale[col // 2, toks, (col % 2) * 128:(col % 2 + 1) * 128]
            hidden = (pre * part * keep).astype(BF)
            slope[col, toks] = (part + pre * jnp.exp(-0.5 * pre * pre) * INV_ROOT_TAU) * keep
            hid[col, toks] = hidden
            put(0, col, g, dot(hidden, wd[col], 1, 0))
        send_group(0, g)

    @pl.loop(0, HALF)
    def _(g):
        @pl.loop(0, XC)
        def _(q):
            wait_slot(tile_in, d_recv, 1, g * XC + q)

        toks = pl.ds(pl.multiple_of(g * GT, GT), GT)
        for col in range(4):
            grad = dot(wide(1, col, g * XC, XC), wd[col], 1, 1)
            grad = (grad * slope[col, toks]).astype(BF)
            gpre[col, toks] = grad
            put(1, col, g, dot(grad, wu[col], 1, 1))
        send_group(1, g)

    @pl.loop(0, 4)
    def _(col):
        grad_up = dot(wide(0, col, 0, ND), gpre[col], 0, 0).astype(BF)
        grad_dn = dot(hid[col], wide(1, col, 0, ND), 0, 0).astype(BF)
        rows = 128 // ZN
        for t in range(ZN):
            for s in range(2):
                gst[t, col, 0, s] = grad_up[s * 128 + t * rows:s * 128 + (t + 1) * rows, :]
                gst[t, col, 1, s] = grad_dn[t * rows:(t + 1) * rows, s * 128:(s + 1) * 128]

    def g_copy(o):
        t = lax.rem(z + o, ZN)
        return remote(gst.at[t], gin_z.at[z], g_send.at[o], g_recv.at[z], blk, t)

    for o in order:
        g_copy(o).start()
    gin_z[z] = gst[z]

    def o_copy(a, t):
        return remote(zo_st.at[a, t], zo_in.at[a, z], o_send.at[a, t], o_recv.at[a, z], blk, t)

    per = ZN // 2
    for a in range(2):
        @pl.loop(0, ND)
        def _(d):
            wait_slot(term_in, t_recv, a, d)

        @pl.loop(0, 2)
        def _(m):
            rows = per * RL * PT
            left = hot[pl.ds(pl.multiple_of(m * rows, rows), rows), :]
            total = dot(left, term_in[a].reshape(ND * 128, 128), 1, 0)
            zo_st[a, pl.ds(m * per, per)] = total.astype(BF).reshape(per, RL, PT, 128)
            for k in range(per):
                t = m * per + k

                @pl.when(t != z)
                def _():
                    o_copy(a, t).start()

        zo_in[a, z] = zo_st[a, z]

        if a == 0:
            for o in order:
                s = lax.rem(z + o, ZN)
                remote(gin_z.at[s], gin_z.at[s], g_send.at[o], g_recv.at[s], blk, z).wait_recv()
            for col in range(4):
                total = gin_z[0, col].astype(F32)
                for s in range(1, ZN):
                    total += gin_z[s, col].astype(F32)
                gsum[col] = total
            there = gsum.at[pl.ds(2 * (1 - up), 2)]
            q_copy = remote(there, gpart, p_send.at[3], p_recv.at[3], partner, z)
            q_copy.start()

    q_copy.wait_recv()
    for cl in range(2):
        own = gsum[2 * up + cl] + gpart[cl]
        for s in range(2):
            live = s < cnt_ref[cl]
            for ref, k in ((gup_ref, 0), (gdn_ref, 1)):
                ref[cl, s] = jnp.where(live, own[k, s], 0.0).astype(BF)

    for a, ref in enumerate((out_ref, gin_ref)):
        for o in order:
            s = lax.rem(z + o, ZN)
            remote(zo_in.at[a, s], zo_in.at[a, s], o_send.at[a, s], o_recv.at[a, s], blk, z).wait_recv()
        for s in range(ZN):
            for i in range(RL):
                ref[s * PT:(s + 1) * PT, i * 128:(i + 1) * 128] = zo_in[a, s, i]

    for o in range(1, XC):
        row_a(o).wait_send()
    for o in range(1, YN):
        row_b(o).wait_send()
    for copy in (*w_copies, m_copy, q_copy):
        copy.wait_send()
    for o in order:
        g_copy(o).wait_send()
        for a in range(2):
            z_copy(a, o).wait_send()
            o_copy(a, lax.rem(z + o, ZN)).wait_send()
    for a in range(2):
        @pl.loop(0, ND)
        def _(i):
            own, far, near = tile_copy(a, i)
            own_t, far_t, near_t = term_copy(a, i)

            @pl.when(jnp.logical_not(own))
            def _():
                far().wait_send()

            @pl.when(jnp.logical_not(own_t))
            def _():
                far_t().wait_send()


def per_device(inputs, grad_out, w_up, w_down, up_rows, slot_counts, keep_mask):
    tok, width = inputs.shape
    zn = lax.axis_size("tp")
    blocks = lax.axis_size("blk")
    xn = X_CHIPS
    yn = blocks // (2 * xn)
    pt, rl = tok // zn, width // 128
    half, xcn = yn // 2, 2 * xn
    nd, gt = half * xcn, xcn * pt
    rows = 128 // zn
    dims = (yn, xn, zn, pt, rl)
    vmem, smem = pl.BlockSpec(memory_space=pltpu.VMEM), pl.BlockSpec(memory_space=pltpu.SMEM)
    V, S = pltpu.VMEM, pltpu.SemaphoreType.DMA
    scratch = [
        V((2, zn, rl, pt, 128), BF),
        V((zn * rl, pt, 128), BF),
        V((zn * rl, pt, 128), BF),
        V((xcn, 8, 128), I32),
        V((yn, 8, 128), I32),
        pltpu.SMEM((yn, 8, 128), I32),
        V((4, 256, 128), BF),
        V((4, 128, 256), BF),
        V((yn, 16, gt), I32),
        V((2, half, 16, gt), I32),
        V((half, 16, gt), I32),
        V((2, half * gt, 256), F32),
        V((2, nd, 8, pt, 128), BF),
        V((2, nd, 8, pt, 128), BF),
        V((4, half * gt, 128), F32),
        V((4, half * gt, 128), BF),
        V((4, half * gt, 128), BF),
        V((2, nd, 8, pt, 128), BF),
        V((2, nd, 8, pt, 128), BF),
        V((nd, 8, 128), I32),
        V((zn * rl * pt, nd * 128), BF),
        V((2, zn, rl, pt, 128), BF),
        V((2, zn, rl, pt, 128), BF),
        V((zn, 4, 2, 2, rows, 128), BF),
        V((zn, 4, 2, 2, rows, 128), BF),
        V((4, 2, 2, rows, 128), F32),
        V((2, 2, 2, rows, 128), F32),
        S((2, zn)), S((2, zn)), S((xcn,)), S((xcn,)), S((yn,)), S((yn,)), S((4,)), S((4,)),
        S((2, nd)), S((2, nd)), S((2, nd)), S((2, nd)), S((2, zn)), S((2, zn)), S((zn,)), S((zn,)), S,
    ]
    shape = jax.ShapeDtypeStruct
    return pl.pallas_call(
        functools.partial(kernel, dims),
        out_shape=(
            shape(inputs.shape, BF), shape(inputs.shape, BF),
            shape((2, 2, rows, 128), BF), shape((2, 2, rows, 128), BF),
        ),
        in_specs=[vmem] * 5 + [smem] * 2,
        out_specs=(vmem,) * 4,
        scratch_shapes=scratch,
        compiler_params=pltpu.CompilerParams(
            collective_id=0, has_side_effects=True, vmem_limit_bytes=48 * 1024 * 1024
        ),
        cost_estimate=pl.CostEstimate(flops=10**10, bytes_accessed=10**7, transcendentals=10**6),
    )(inputs, grad_out, w_up, w_down, keep_mask.T, up_rows, slot_counts)


def solution(mesh):
    return jax.shard_map(
        per_device,
        mesh=mesh,
        in_specs=(
            P("blk", "tp"),
            P("blk", "tp"),
            P("blk", None, None, None),
            P("blk", None, None, None),
            P("blk", None),
            P("blk"),
            P(None, "blk"),
        ),
        out_specs=(
            P("blk", "tp"),
            P("blk", "tp"),
            P("blk", None, "tp", None),
            P("blk", None, "tp", None),
        ),
        check_vma=False,
    )
```

```python
import functools

import jax
import jax.numpy as jnp
from jax import lax
from jax.experimental import pallas as pl
from jax.experimental.pallas import tpu as pltpu
from jax.sharding import PartitionSpec as P

INV_ROOT_TWO = 0.7071067811865476
INV_ROOT_TAU = 0.3989422804014327
KEEP_SCALE = 1.25
MESH = pl.DeviceIdType.MESH
X_CHIPS = 4
BF = jnp.bfloat16
F32 = jnp.float32
I32 = jnp.int32


def dot(a, b, ca, cb):
    return lax.dot_general(a, b, (((ca,), (cb,)), ((), ())), preferred_element_type=F32)


def iota(shape, dim):
    return lax.broadcasted_iota(I32, shape, dim)


def hop(value, step, count):
    there = value + step
    there = jnp.where(there >= count, there - count, there)
    return jnp.where(there < 0, there + count, there)


def split(value, count):
    shift = count.bit_length() - 1
    assert count == 1 << shift
    return jnp.right_shift(value, shift), jnp.bitwise_and(value, count - 1)


def kernel(
    dims,
    x_hbm, dy_hbm, wu_hbm, wd_hbm, keep_hbm, rows_ref, cnt_ref,
    out_ref, gin_ref, gup_ref, gdn_ref,
    x_ref, dy_ref, wu_ref, wd_ref, keep_ref, zst, full_x, full_dy, rows_a, rows_b, rows_s, wu, wd, tokw, maskw, mask_st, scale,
    tile_st, tile_in, slope, hid, gpre, term_st, term_in, lanes, hot,
    zo_st, zo_in, gst, gin_z, gsum, gpart,
    z_send, z_recv, a_send, a_recv, b_send, b_recv, p_send, p_recv,
    d_send, d_recv, t_send, t_recv, o_send, o_recv, g_send, g_recv, l_sem, in_sem, v_send, v_recv,
):
    YN, XN, ZN, PT, RL = dims
    XC = XN * 2
    HALF = YN // 2
    LO = HALF // 2 - 1
    ND = HALF * XC
    RB = RL * ZN
    GT = XC * PT
    blk, z = lax.axis_index("blk"), lax.axis_index("tp")
    c = lax.rem(blk, 2)
    x = lax.rem(blk // 2, XN)
    y = blk // XC
    xc = x * 2 + c
    up = jnp.where(y >= HALF, 1, 0)
    partner = hop(y, HALF, YN) * XC + xc

    def remote(src, dst, ss, rs, b, t):
        return pltpu.make_async_remote_copy(
            src_ref=src, dst_ref=dst, send_sem=ss, recv_sem=rs, device_id=(b, t), device_id_type=MESH
        )

    fetch = [
        pltpu.make_async_copy(src, dst, in_sem.at[k])
        for k, (src, dst) in enumerate(
            ((x_hbm, x_ref), (dy_hbm, dy_ref), (wu_hbm, wu_ref), (wd_hbm, wd_ref), (keep_hbm, keep_ref))
        )
    ]
    for one in fetch:
        one.start()

    barrier = pltpu.get_barrier_semaphore()
    peers = []
    for dy in range(-(HALF // 2), YN - HALF // 2):
        for xo in range(XN):
            for co in range(2):
                if (dy, xo, co) == (0, 0, 0):
                    continue
                if abs(dy) <= HALF // 2 or (xo, co) == (0, 0):
                    peers.append((hop(y, dy, YN) * XC + hop(x, xo, XN) * 2 + hop(c, co, 2), z))
    for zo in range(1, ZN):
        peers.append((blk, hop(z, zo, ZN)))
    for b, t in peers:
        pl.semaphore_signal(barrier, inc=1, device_id=(b, t), device_id_type=MESH)

    full = (full_x, full_dy)
    lane = iota((8, 128), 1)
    mine = jnp.where(lane == 0, rows_ref[0, 0], jnp.where(lane == 1, rows_ref[0, 1],
                     jnp.where(lane == 2, rows_ref[1, 0], rows_ref[1, 1])))
    rows_a[xc] = mine
    for a, ref in enumerate((x_ref, dy_ref)):
        fetch[a].wait()
        for t in range(ZN):
            for i in range(RL):
                zst[a, t, i] = ref[t * PT:(t + 1) * PT, i * 128:(i + 1) * 128]
        full[a][pl.ds(z * RL, RL)] = zst[a, z]
    fetch[2].wait()
    fetch[3].wait()
    for cl in range(2):
        for s in range(2):
            live = s < cnt_ref[cl]
            wu[2 * up + cl, s * 128:(s + 1) * 128, :] = jnp.where(live, wu_ref[cl, s], jnp.zeros((), BF))
            wd[2 * up + cl, :, s * 128:(s + 1) * 128] = jnp.where(live, wd_ref[cl, s], jnp.zeros((), BF))
    pl.semaphore_wait(barrier, len(peers))

    def row_a(o):
        q = hop(xc, o, XC)
        return remote(rows_a.at[xc], rows_a.at[xc], a_send.at[o], a_recv.at[xc], y * XC + q, z)

    for o in range(1, XC):
        row_a(o).start()

    order = [o for k in range(1, ZN // 2 + 1) for o in dict.fromkeys((k, ZN - k))]

    def z_copy(a, o):
        t = hop(z, o, ZN)
        return remote(zst.at[a, t], full[a].at[pl.ds(z * RL, RL)], z_send.at[a], z_recv.at[a], blk, t)

    for o in order:
        z_copy(0, o).start()

    def w_slice(k, half, at):
        rows = (256, 128)[k] // ZN
        return (wu, wd)[k].at[pl.ds(2 * half, 2), pl.ds(pl.multiple_of(at * rows, rows), rows)]

    w_copies = [
        remote(w_slice(k, up, z), w_slice(k, up, z), p_send.at[k], p_recv.at[k], partner, z) for k in range(2)
    ]
    for w_copy in w_copies:
        w_copy.start()

    def wait_a(o):
        q = hop(xc, o, XC)
        remote(rows_a.at[q], rows_a.at[q], a_send.at[o], a_recv.at[q], blk, z).wait_recv()

    for o in range(1, XC):
        wait_a(o)
    sub = iota((8, 128), 0)
    packed = rows_a[0]
    for q in range(1, XC):
        packed = jnp.where(sub == q, rows_a[q], packed)
    rows_b[y] = packed

    def row_b(o):
        q = hop(y, o, YN)
        return remote(rows_b.at[y], rows_b.at[y], b_send.at[o], b_recv.at[y], q * XC + xc, z)

    for o in range(1, YN):
        row_b(o).start()
    for o in range(1, YN):
        q = hop(y, o, YN)
        remote(rows_b.at[q], rows_b.at[q], b_send.at[o], b_recv.at[q], blk, z).wait_recv()
    to_scalar = pltpu.make_async_copy(rows_b, rows_s, l_sem)
    to_scalar.start()
    to_scalar.wait()

    def token_side(j, xo, co):
        xd, cd = hop(x, xo, XN), hop(c, co, 2)
        yd = hop(y, LO - j + cd, YN)
        return j * XC + xd * 2 + cd, yd, xd * 2 + cd, j * XC + xc

    def owner_side(j, xo, co):
        xd, cd = hop(x, xo, XN), hop(c, co, 2)
        yd = hop(y, j - LO - c, YN)
        return j * XC + xd * 2 + cd, yd, xd * 2 + cd, j * XC + xc

    def send_to(side, st, into, sends, recvs, a, j, xo, co):
        d, yd, xcd, at = side(j, xo, co)
        own = (j == LO + c) & (xo == 0)

        def near():
            pltpu.make_async_copy(st.at[a, d], into.at[a, at], recvs.at[a, j]).start()

        def far():
            remote(st.at[a, d], into.at[a, at], sends.at[a], recvs.at[a, j], yd * XC + xcd, z).start()

        if co == 0:
            pl.when(own)(near)
            pl.when(jnp.logical_not(own))(far)
        else:
            far()

    def slot_rows(yd, xcd):
        low = jnp.where(yd >= HALF, yd - HALF, yd)
        return [rows_s[low + HALF * (k // 4), xcd, k % 4] for k in range(8)]

    def wait_z(a):
        others = full[a].at[pl.ds(0, (ZN - 1) * RL)]
        remote(others, others, z_send.at[a], z_recv.at[a], blk, z).wait_recv()

    def dispatch(a):
        @pl.loop(0, XN)
        def _(xo):
            for co in range(2):
                for j in range(HALF):
                    d, yd, xcd, at = token_side(j, xo, co)
                    for k, row in enumerate(slot_rows(yd, xcd)):
                        tile_st[a, d, k] = full[a][row]
                    send_to(token_side, tile_st, tile_in, d_send, d_recv, a, j, xo, co)

    wait_z(0)
    for o in order:
        z_copy(1, o).start()
    for k in range(2):
        mine = w_slice(k, 1 - up, z)
        remote(mine, mine, p_send.at[k], p_recv.at[k], partner, z).wait_recv()
        for o in order:
            remote(mine, mine, v_send.at[k], v_recv.at[k], blk, hop(z, o, ZN)).start()
    dispatch(0)

    span = XC * ZN * PT
    r, l = iota((span, GT), 0), iota((span, GT), 1)
    share = ZN * PT
    (r, rest), (l, near) = split(r, share), split(l, PT)
    pick = jnp.where((r == l) & (rest == z * PT + near), 1.0, 0.0).astype(BF)
    fetch[4].wait()
    for g in range(YN):
        words = keep_ref[:, g * span:(g + 1) * span]
        low = jnp.bitwise_and(words, 255).astype(F32).astype(BF)
        high = jnp.right_shift(words, 8).astype(F32).astype(BF)
        found = dot(jnp.concatenate([low, high], axis=0), pick, 1, 0).astype(I32)
        tokw[g] = found[:16] + found[16:] * 256
    for j in range(HALF):
        maskw[up, j] = tokw[hop(y, j - LO - c, YN)]
        mask_st[j] = tokw[hop(hop(y, HALF, YN), j - LO - c, YN)]
    m_copy = remote(mask_st, maskw.at[up], p_send.at[2], p_recv.at[2], partner, z)
    m_copy.start()

    wait_z(1)
    dispatch(1)

    piece, near_token = split(lane, PT)

    @pl.loop(0, XN)
    def _(xo):
        for co in range(2):
            for j in range(HALF):
                d, yd, xcd, at = token_side(j, xo, co)
                value = near_token
                for k, row in enumerate(slot_rows(yd, xcd)):
                    value = jnp.where(piece == k, row * PT + near_token, value)
                lanes[d] = value

    @pl.loop(0, ND)
    def _(d):
        want = lanes[d][0:1, :]
        at = pl.ds(pl.multiple_of(d * 128, 128), 128)
        hot[:, at] = jnp.where(iota((RB * PT, 128), 0) == want, 1.0, 0.0).astype(BF)

    m_wait = remote(mask_st, maskw.at[1 - up], p_send.at[2], p_recv.at[2], partner, z)
    m_wait.wait_recv()
    er, el = iota((32, 256), 0), iota((32, 256), 1)
    (word, bit), (_, which) = split(el, 16), split(er, 16)
    spread = jnp.where((word == which) & ((bit >= 8) == (er >= 16)), 1.0, 0.0).astype(BF)
    shift = split(iota((GT, 256), 1), 8)[1]
    for h in range(2):
        for j in range(HALF):
            words = maskw[h, j]
            low = jnp.bitwise_and(words, 255).astype(F32).astype(BF)
            high = jnp.right_shift(words, 8).astype(F32).astype(BF)
            found = dot(jnp.concatenate([low, high], axis=0), spread, 0, 0).astype(I32)
            keep = jnp.bitwise_and(jnp.right_shift(found, shift), 1)
            scale[h, j * GT:(j + 1) * GT, :] = keep.astype(F32) * KEEP_SCALE
    def seven(k):
        rows = (256, 128)[k] // ZN
        return (wu, wd)[k].at[pl.ds(0, 2), pl.ds(0, (ZN - 1) * rows)]

    for k in range(2):
        remote(seven(k), seven(k), v_send.at[k], v_recv.at[k], blk, z).wait_recv()

    def wide(a, col, start, count):
        parts = [tile_in[a, pl.ds(start, count), 2 * col + s].reshape(count * PT, 128) for s in range(2)]
        return jnp.concatenate(parts, axis=1)

    def wait_group(buf, sem, a, g):
        block = buf.at[a, pl.ds(g * XC, XC)]
        remote(block, block, sem.at[a, g], sem.at[a, g], blk, z).wait_recv()

    def put(a, col, g, value):
        value = value.astype(BF)
        for s in range(2):
            term_st[a, pl.ds(g * XC, XC), 2 * col + s] = value[:, s * 128:(s + 1) * 128].reshape(XC, PT, 128)

    def send_group(a, g):
        @pl.loop(0, XN)
        def _(xo):
            for co in range(2):
                send_to(owner_side, term_st, term_in, t_send, t_recv, a, g, xo, co)

    @pl.loop(0, HALF)
    def _(g):
        wait_group(tile_in, d_recv, 0, g)
        toks = pl.ds(pl.multiple_of(g * GT, GT), GT)
        for col in range(4):
            pre = dot(wide(0, col, g * XC, XC), wu[col], 1, 0)
            part = 0.5 * (1.0 + lax.erf(pre * INV_ROOT_TWO))
            keep = scale[col // 2, toks, (col % 2) * 128:(col % 2 + 1) * 128]
            hidden = (pre * part * keep).astype(BF)
            slope[col, toks] = (part + pre * jnp.exp(-0.5 * pre * pre) * INV_ROOT_TAU) * keep
            hid[col, toks] = hidden
            put(0, col, g, dot(hidden, wd[col], 1, 0))
        send_group(0, g)

    @pl.loop(0, HALF)
    def _(g):
        wait_group(tile_in, d_recv, 1, g)
        toks = pl.ds(pl.multiple_of(g * GT, GT), GT)
        for col in range(4):
            grad = dot(wide(1, col, g * XC, XC), wd[col], 1, 1)
            grad = (grad * slope[col, toks]).astype(BF)
            gpre[col, toks] = grad
            put(1, col, g, dot(grad, wu[col], 1, 1))
        send_group(1, g)

    @pl.loop(0, 4)
    def _(col):
        grad_up = dot(wide(0, col, 0, ND), gpre[col], 0, 0).astype(BF)
        grad_dn = dot(hid[col], wide(1, col, 0, ND), 0, 0).astype(BF)
        rows = 128 // ZN
        for t in range(ZN):
            for s in range(2):
                gst[t, col, 0, s] = grad_up[s * 128 + t * rows:s * 128 + (t + 1) * rows, :]
                gst[t, col, 1, s] = grad_dn[t * rows:(t + 1) * rows, s * 128:(s + 1) * 128]

    def g_copy(o):
        t = hop(z, o, ZN)
        return remote(gst.at[t], gin_z.at[z], g_send, g_recv, blk, t)

    for o in order:
        g_copy(o).start()
    gin_z[z] = gst[z]

    def o_copy(a, t):
        return remote(zo_st.at[a, t], zo_in.at[a, z], o_send.at[a], o_recv.at[a], blk, t)

    per = ZN // 2
    for a in range(2):
        for j in range(HALF):
            wait_group(term_in, t_recv, a, j)

        @pl.loop(0, 2)
        def _(m):
            rows = per * RL * PT
            left = hot[pl.ds(pl.multiple_of(m * rows, rows), rows), :]
            total = dot(left, term_in[a].reshape(ND * 128, 128), 1, 0)
            zo_st[a, pl.ds(m * per, per)] = total.astype(BF).reshape(per, RL, PT, 128)
            for k in range(per):
                t = m * per + k

                @pl.when(t != z)
                def _():
                    o_copy(a, t).start()

        zo_in[a, z] = zo_st[a, z]

    most = pl.ds(0, ZN - 1)
    remote(gin_z.at[most], gin_z.at[most], g_send, g_recv, blk, z).wait_recv()
    for col in range(4):
        total = gin_z[0, col].astype(F32)
        for s in range(1, ZN):
            total += gin_z[s, col].astype(F32)
        gsum[col] = total
    there = gsum.at[pl.ds(2 * (1 - up), 2)]
    q_copy = remote(there, gpart, p_send.at[3], p_recv.at[3], partner, z)
    q_copy.start()

    for a, ref in enumerate((out_ref, gin_ref)):
        remote(zo_in.at[a, most], zo_in.at[a, most], o_send.at[a], o_recv.at[a], blk, z).wait_recv()
        for s in range(ZN):
            for i in range(RL):
                ref[s * PT:(s + 1) * PT, i * 128:(i + 1) * 128] = zo_in[a, s, i]

    q_copy.wait_recv()
    for cl in range(2):
        own = gsum[2 * up + cl] + gpart[cl]
        for s in range(2):
            live = s < cnt_ref[cl]
            for ref, k in ((gup_ref, 0), (gdn_ref, 1)):
                ref[cl, s] = jnp.where(live, own[k, s], 0.0).astype(BF)

    for o in range(1, XC):
        row_a(o).wait_send()
    for o in range(1, YN):
        row_b(o).wait_send()
    for copy in (*w_copies, m_copy, q_copy):
        copy.wait_send()
    sent = pl.ds(0, ND - 1)
    for a in range(2):
        for buf, sem in (
            (zst.at[a, most], z_send), (zo_st.at[a, most], o_send),
            (tile_st.at[a, sent], d_send), (term_st.at[a, sent], t_send),
        ):
            remote(buf, buf, sem.at[a], sem.at[a], blk, z).wait_send()
    remote(gst.at[most], gst.at[most], g_send, g_recv, blk, z).wait_send()
    for k in range(2):
        remote(seven(k), seven(k), v_send.at[k], v_recv.at[k], blk, z).wait_send()


def place(*refs):
    for src, dst in zip(refs[:4], refs[4:]):
        dst[...] = src[...]


def per_device(inputs, grad_out, w_up, w_down, up_rows, slot_counts, keep_mask):
    tok, width = inputs.shape
    zn = lax.axis_size("tp")
    blocks = lax.axis_size("blk")
    xn = X_CHIPS
    yn = blocks // (2 * xn)
    pt, rl = tok // zn, width // 128
    half, xcn = yn // 2, 2 * xn
    nd, gt = half * xcn, xcn * pt
    rows = 128 // zn
    dims = (yn, xn, zn, pt, rl)
    vmem, smem = pl.BlockSpec(memory_space=pltpu.VMEM), pl.BlockSpec(memory_space=pltpu.SMEM)
    V, S = pltpu.VMEM, pltpu.SemaphoreType.DMA
    scratch = [
        V(inputs.shape, BF), V(inputs.shape, BF), V(w_up.shape, BF), V(w_down.shape, BF),
        V(keep_mask.shape[::-1], I32),
        V((2, zn, rl, pt, 128), BF),
        V((zn * rl, pt, 128), BF),
        V((zn * rl, pt, 128), BF),
        V((xcn, 8, 128), I32),
        V((yn, 8, 128), I32),
        pltpu.SMEM((yn, 8, 128), I32),
        V((4, 256, 128), BF),
        V((4, 128, 256), BF),
        V((yn, 16, gt), I32),
        V((2, half, 16, gt), I32),
        V((half, 16, gt), I32),
        V((2, half * gt, 256), F32),
        V((2, nd, 8, pt, 128), BF),
        V((2, nd, 8, pt, 128), BF),
        V((4, half * gt, 128), F32),
        V((4, half * gt, 128), BF),
        V((4, half * gt, 128), BF),
        V((2, nd, 8, pt, 128), BF),
        V((2, nd, 8, pt, 128), BF),
        V((nd, 8, 128), I32),
        V((zn * rl * pt, nd * 128), BF),
        V((2, zn, rl, pt, 128), BF),
        V((2, zn, rl, pt, 128), BF),
        V((zn, 4, 2, 2, rows, 128), BF),
        V((zn, 4, 2, 2, rows, 128), BF),
        V((4, 2, 2, rows, 128), F32),
        V((2, 2, 2, rows, 128), F32),
        S((2,)), S((2,)), S((xcn,)), S((xcn,)), S((yn,)), S((yn,)), S((4,)), S((4,)),
        S((2,)), S((2, half)), S((2,)), S((2, half)), S((2,)), S((2,)), S, S, S, S((5,)), S((2,)), S((2,)),
    ]
    shape = jax.ShapeDtypeStruct
    shapes = (
        shape(inputs.shape, BF), shape(inputs.shape, BF),
        shape((2, 2, rows, 128), BF), shape((2, 2, rows, 128), BF),
    )
    results = pl.pallas_call(
        functools.partial(kernel, dims),
        out_shape=shapes,
        in_specs=[pl.BlockSpec(memory_space=pl.ANY)] * 5 + [smem] * 2,
        out_specs=(vmem,) * 4,
        scratch_shapes=scratch,
        compiler_params=pltpu.CompilerParams(
            collective_id=0, has_side_effects=True, vmem_limit_bytes=56 * 1024 * 1024
        ),
        cost_estimate=pl.CostEstimate(flops=10**10, bytes_accessed=10**7, transcendentals=10**6),
    )(inputs, grad_out, w_up, w_down, keep_mask.T, up_rows, slot_counts)
    return pl.pallas_call(place, out_shape=shapes, in_specs=[vmem] * 4, out_specs=(vmem,) * 4)(*results)


def solution(mesh):
    return jax.shard_map(
        per_device,
        mesh=mesh,
        in_specs=(
            P("blk", "tp"),
            P("blk", "tp"),
            P("blk", None, None, None),
            P("blk", None, None, None),
            P("blk", None),
            P("blk"),
            P(None, "blk"),
        ),
        out_specs=(
            P("blk", "tp"),
            P("blk", "tp"),
            P("blk", None, "tp", None),
            P("blk", None, "tp", None),
        ),
        check_vma=False,
    )
```

```python
import functools

import jax
import jax.numpy as jnp
from jax import lax
from jax.experimental import pallas as pl
from jax.experimental.pallas import tpu as pltpu
from jax.sharding import PartitionSpec as P

INV_ROOT_TWO = 0.7071067811865476
INV_ROOT_TAU = 0.3989422804014327
KEEP_SCALE = 1.25
MESH = pl.DeviceIdType.MESH
X_CHIPS = 4
BF = jnp.bfloat16
F32 = jnp.float32
I32 = jnp.int32


def dot(a, b, ca, cb):
    return lax.dot_general(a, b, (((ca,), (cb,)), ((), ())), preferred_element_type=F32)


def iota(shape, dim):
    return lax.broadcasted_iota(I32, shape, dim)


def hop(value, step, count):
    there = value + step
    there = jnp.where(there >= count, there - count, there)
    return jnp.where(there < 0, there + count, there)


def split(value, count):
    shift = count.bit_length() - 1
    assert count == 1 << shift
    return jnp.right_shift(value, shift), jnp.bitwise_and(value, count - 1)


def kernel(
    dims,
    x_hbm, dy_hbm, wu_hbm, wd_hbm, keep_hbm, rows_ref, cnt_ref,
    out_ref, gin_ref, gup_ref, gdn_ref,
    x_ref, dy_ref, wu_ref, wd_ref, keep_ref, zst, full_x, full_dy, rows_a, rows_b, rows_s, wu, wd, tokw, maskw, mask_st, scale,
    tile_st, tile_in, slope, hid, gpre, term_st, term_in, lanes, hot,
    acc, zo_st, zo_in, gst, gin_z, gsum, gpart,
    z_send, z_recv, a_send, a_recv, b_send, b_recv, p_send, p_recv,
    d_send, d_recv, t_send, t_recv, o_send, o_recv, g_send, g_recv, l_sem, in_sem, v_send, v_recv,
):
    YN, XN, ZN, PT, RL = dims
    XC = XN * 2
    HALF = YN // 2
    LO = HALF // 2 - 1
    ND = HALF * XC
    RB = RL * ZN
    GT = XC * PT
    blk, z = lax.axis_index("blk"), lax.axis_index("tp")
    c = lax.rem(blk, 2)
    x = lax.rem(blk // 2, XN)
    y = blk // XC
    xc = x * 2 + c
    up = jnp.where(y >= HALF, 1, 0)
    partner = hop(y, HALF, YN) * XC + xc

    def remote(src, dst, ss, rs, b, t):
        return pltpu.make_async_remote_copy(
            src_ref=src, dst_ref=dst, send_sem=ss, recv_sem=rs, device_id=(b, t), device_id_type=MESH
        )

    fetch = [
        pltpu.make_async_copy(src, dst, in_sem.at[k])
        for k, (src, dst) in enumerate(
            ((x_hbm, x_ref), (dy_hbm, dy_ref), (wu_hbm, wu_ref), (wd_hbm, wd_ref), (keep_hbm, keep_ref))
        )
    ]
    for one in fetch:
        one.start()

    barrier = pltpu.get_barrier_semaphore()
    peers = []
    for dy in range(-(HALF // 2), YN - HALF // 2):
        for xo in range(XN):
            for co in range(2):
                if (dy, xo, co) == (0, 0, 0):
                    continue
                if abs(dy) <= HALF // 2 or (xo, co) == (0, 0):
                    peers.append((hop(y, dy, YN) * XC + hop(x, xo, XN) * 2 + hop(c, co, 2), z))
    for zo in range(1, ZN):
        peers.append((blk, hop(z, zo, ZN)))
    for b, t in peers:
        pl.semaphore_signal(barrier, inc=1, device_id=(b, t), device_id_type=MESH)

    full = (full_x, full_dy)
    lane = iota((8, 128), 1)
    mine = jnp.where(lane == 0, rows_ref[0, 0], jnp.where(lane == 1, rows_ref[0, 1],
                     jnp.where(lane == 2, rows_ref[1, 0], rows_ref[1, 1])))
    rows_a[xc] = mine
    for a, ref in enumerate((x_ref, dy_ref)):
        fetch[a].wait()
        for t in range(ZN):
            for i in range(RL):
                zst[a, t, i] = ref[t * PT:(t + 1) * PT, i * 128:(i + 1) * 128]
        full[a][pl.ds(z * RL, RL)] = zst[a, z]
    fetch[2].wait()
    fetch[3].wait()
    for cl in range(2):
        for s in range(2):
            live = s < cnt_ref[cl]
            wu[2 * up + cl, s * 128:(s + 1) * 128, :] = jnp.where(live, wu_ref[cl, s], jnp.zeros((), BF))
            wd[2 * up + cl, :, s * 128:(s + 1) * 128] = jnp.where(live, wd_ref[cl, s], jnp.zeros((), BF))
    pl.semaphore_wait(barrier, len(peers))

    def row_a(o):
        q = hop(xc, o, XC)
        return remote(rows_a.at[xc], rows_a.at[xc], a_send.at[o], a_recv.at[xc], y * XC + q, z)

    for o in range(1, XC):
        row_a(o).start()

    order = [o for k in range(1, ZN // 2 + 1) for o in dict.fromkeys((k, ZN - k))]

    def z_copy(a, o):
        t = hop(z, o, ZN)
        return remote(zst.at[a, t], full[a].at[pl.ds(z * RL, RL)], z_send.at[a], z_recv.at[a], blk, t)

    for o in order:
        z_copy(0, o).start()

    def w_slice(k, half, at):
        rows = (256, 128)[k] // ZN
        return (wu, wd)[k].at[pl.ds(2 * half, 2), pl.ds(pl.multiple_of(at * rows, rows), rows)]

    w_copies = [
        remote(w_slice(k, up, z), w_slice(k, up, z), p_send.at[k], p_recv.at[k], partner, z) for k in range(2)
    ]
    for w_copy in w_copies:
        w_copy.start()

    def wait_a(o):
        q = hop(xc, o, XC)
        remote(rows_a.at[q], rows_a.at[q], a_send.at[o], a_recv.at[q], blk, z).wait_recv()

    for o in range(1, XC):
        wait_a(o)
    sub = iota((8, 128), 0)
    packed = rows_a[0]
    for q in range(1, XC):
        packed = jnp.where(sub == q, rows_a[q], packed)
    rows_b[y] = packed

    def row_b(o):
        q = hop(y, o, YN)
        return remote(rows_b.at[y], rows_b.at[y], b_send.at[o], b_recv.at[y], q * XC + xc, z)

    for o in range(1, YN):
        row_b(o).start()
    for o in range(1, YN):
        q = hop(y, o, YN)
        remote(rows_b.at[q], rows_b.at[q], b_send.at[o], b_recv.at[q], blk, z).wait_recv()
    to_scalar = pltpu.make_async_copy(rows_b, rows_s, l_sem)
    to_scalar.start()
    to_scalar.wait()

    x_order = [xo for xo in (2, 1, 0, 3) if xo < XN]

    def token_side(j, xo, co):
        xd, cd = hop(x, xo, XN), hop(c, co, 2)
        yd = hop(y, LO - j + cd, YN)
        return j * XC + xd * 2 + cd, yd, xd * 2 + cd, j * XC + xc

    def owner_side(j, xo, co):
        xd, cd = hop(x, xo, XN), hop(c, co, 2)
        yd = hop(y, j - LO - c, YN)
        return j * XC + xd * 2 + cd, yd, xd * 2 + cd, j * XC + xc

    def send_to(side, st, into, sends, recvs, a, j, xo, co):
        d, yd, xcd, at = side(j, xo, co)
        own = j == LO + c

        def near():
            pltpu.make_async_copy(st.at[a, d], into.at[a, at], recvs.at[a, j]).start()

        def far():
            remote(st.at[a, d], into.at[a, at], sends.at[a], recvs.at[a, j], yd * XC + xcd, z).start()

        if co == 0 and xo == 0:
            pl.when(own)(near)
            pl.when(jnp.logical_not(own))(far)
        else:
            far()

    def slot_rows(yd, xcd):
        low = jnp.where(yd >= HALF, yd - HALF, yd)
        return [rows_s[low + HALF * (k // 4), xcd, k % 4] for k in range(8)]

    def wait_z(a):
        others = full[a].at[pl.ds(0, (ZN - 1) * RL)]
        remote(others, others, z_send.at[a], z_recv.at[a], blk, z).wait_recv()

    def dispatch(a):
        @pl.loop(0, HALF)
        def _(j):
            for co in range(2):
                for xo in x_order:
                    d, yd, xcd, at = token_side(j, xo, co)
                    for k, row in enumerate(slot_rows(yd, xcd)):
                        tile_st[a, d, k] = full[a][row]
                    send_to(token_side, tile_st, tile_in, d_send, d_recv, a, j, xo, co)

    wait_z(0)
    for o in order:
        z_copy(1, o).start()
    for k in range(2):
        mine = w_slice(k, 1 - up, z)
        remote(mine, mine, p_send.at[k], p_recv.at[k], partner, z).wait_recv()
        for o in order:
            remote(mine, mine, v_send.at[k], v_recv.at[k], blk, hop(z, o, ZN)).start()
    dispatch(0)

    span = XC * ZN * PT
    r, l = iota((span, GT), 0), iota((span, GT), 1)
    share = ZN * PT
    (r, rest), (l, near) = split(r, share), split(l, PT)
    pick = jnp.where((r == l) & (rest == z * PT + near), 1.0, 0.0).astype(BF)
    fetch[4].wait()
    for g in range(YN):
        words = keep_ref[:, g * span:(g + 1) * span]
        low = jnp.bitwise_and(words, 255).astype(F32).astype(BF)
        high = jnp.right_shift(words, 8).astype(F32).astype(BF)
        found = dot(jnp.concatenate([low, high], axis=0), pick, 1, 0).astype(I32)
        tokw[g] = found[:16] + found[16:] * 256
    for j in range(HALF):
        maskw[up, j] = tokw[hop(y, j - LO - c, YN)]
        mask_st[j] = tokw[hop(hop(y, HALF, YN), j - LO - c, YN)]
    m_copy = remote(mask_st, maskw.at[up], p_send.at[2], p_recv.at[2], partner, z)
    m_copy.start()

    wait_z(1)
    dispatch(1)

    piece, near_token = split(lane, PT)

    @pl.loop(0, XN)
    def _(xo):
        for co in range(2):
            for j in range(HALF):
                d, yd, xcd, at = token_side(j, xo, co)
                value = near_token
                for k, row in enumerate(slot_rows(yd, xcd)):
                    value = jnp.where(piece == k, row * PT + near_token, value)
                lanes[d] = value

    @pl.loop(0, ND)
    def _(d):
        want = lanes[d][0:1, :]
        at = pl.ds(pl.multiple_of(d * 128, 128), 128)
        hot[:, at] = jnp.where(iota((RB * PT, 128), 0) == want, 1.0, 0.0).astype(BF)

    m_wait = remote(mask_st, maskw.at[1 - up], p_send.at[2], p_recv.at[2], partner, z)
    m_wait.wait_recv()
    er, el = iota((32, 256), 0), iota((32, 256), 1)
    (word, bit), (_, which) = split(el, 16), split(er, 16)
    spread = jnp.where((word == which) & ((bit >= 8) == (er >= 16)), 1.0, 0.0).astype(BF)
    shift = split(iota((GT, 256), 1), 8)[1]
    for h in range(2):
        for j in range(HALF):
            words = maskw[h, j]
            low = jnp.bitwise_and(words, 255).astype(F32).astype(BF)
            high = jnp.right_shift(words, 8).astype(F32).astype(BF)
            found = dot(jnp.concatenate([low, high], axis=0), spread, 0, 0).astype(I32)
            keep = jnp.bitwise_and(jnp.right_shift(found, shift), 1)
            scale[h, j * GT:(j + 1) * GT, :] = keep.astype(F32) * KEEP_SCALE
    def seven(k):
        rows = (256, 128)[k] // ZN
        return (wu, wd)[k].at[pl.ds(0, 2), pl.ds(0, (ZN - 1) * rows)]

    for k in range(2):
        remote(seven(k), seven(k), v_send.at[k], v_recv.at[k], blk, z).wait_recv()

    def wide(a, col, start, count):
        parts = [tile_in[a, pl.ds(start, count), 2 * col + s].reshape(count * PT, 128) for s in range(2)]
        return jnp.concatenate(parts, axis=1)

    def wait_group(buf, sem, a, g):
        block = buf.at[a, pl.ds(g * XC, XC)]
        remote(block, block, sem.at[a, g], sem.at[a, g], blk, z).wait_recv()

    def put(a, col, g, value):
        value = value.astype(BF)
        for s in range(2):
            term_st[a, pl.ds(g * XC, XC), 2 * col + s] = value[:, s * 128:(s + 1) * 128].reshape(XC, PT, 128)

    def send_group(a, g):
        for co in range(2):
            for xo in x_order:
                send_to(owner_side, term_st, term_in, t_send, t_recv, a, g, xo, co)

    @pl.loop(0, HALF)
    def _(g):
        wait_group(tile_in, d_recv, 0, g)
        toks = pl.ds(pl.multiple_of(g * GT, GT), GT)
        for col in range(4):
            pre = dot(wide(0, col, g * XC, XC), wu[col], 1, 0)
            part = 0.5 * (1.0 + lax.erf(pre * INV_ROOT_TWO))
            keep = scale[col // 2, toks, (col % 2) * 128:(col % 2 + 1) * 128]
            hidden = (pre * part * keep).astype(BF)
            slope[col, toks] = (part + pre * jnp.exp(-0.5 * pre * pre) * INV_ROOT_TAU) * keep
            hid[col, toks] = hidden
            put(0, col, g, dot(hidden, wd[col], 1, 0))
        send_group(0, g)

    @pl.loop(0, HALF)
    def _(g):
        wait_group(tile_in, d_recv, 1, g)
        toks = pl.ds(pl.multiple_of(g * GT, GT), GT)
        for col in range(4):
            grad = dot(wide(1, col, g * XC, XC), wd[col], 1, 1)
            grad = (grad * slope[col, toks]).astype(BF)
            gpre[col, toks] = grad
            put(1, col, g, dot(grad, wu[col], 1, 1))
        send_group(1, g)

    @pl.loop(0, 4)
    def _(col):
        grad_up = dot(wide(0, col, 0, ND), gpre[col], 0, 0).astype(BF)
        grad_dn = dot(hid[col], wide(1, col, 0, ND), 0, 0).astype(BF)
        rows = 128 // ZN
        for t in range(ZN):
            for s in range(2):
                gst[t, col, 0, s] = grad_up[s * 128 + t * rows:s * 128 + (t + 1) * rows, :]
                gst[t, col, 1, s] = grad_dn[t * rows:(t + 1) * rows, s * 128:(s + 1) * 128]

    def g_copy(o):
        t = hop(z, o, ZN)
        return remote(gst.at[t], gin_z.at[z], g_send, g_recv, blk, t)

    for o in order:
        g_copy(o).start()
    gin_z[z] = gst[z]

    def o_copy(a, t):
        return remote(zo_st.at[a, t], zo_in.at[a, z], o_send.at[a], o_recv.at[a], blk, t)

    rows = RL * PT
    deep = XC * 128

    def chosen(a, g, t, count):
        left = hot[pl.ds(pl.multiple_of(t * rows, rows), count * rows), pl.ds(pl.multiple_of(g * deep, deep), deep)]
        return dot(left, term_in[a, pl.ds(g * XC, XC)].reshape(deep, 128), 1, 0)

    for a in range(2):
        wait_group(term_in, t_recv, a, 0)

        @pl.loop(0, ZN // 2)
        def _(m):
            acc[pl.ds(pl.multiple_of(m * 2 * rows, rows), 2 * rows)] = chosen(a, 0, 2 * m, 2)

        @pl.loop(1, HALF - 1)
        def _(g):
            wait_group(term_in, t_recv, a, g)

            @pl.loop(0, ZN // 2)
            def _(m):
                acc[pl.ds(pl.multiple_of(m * 2 * rows, rows), 2 * rows)] += chosen(a, g, 2 * m, 2)

        wait_group(term_in, t_recv, a, HALF - 1)
        for o in (*order[::-1], 0):
            t = hop(z, o, ZN)
            total = acc[pl.ds(pl.multiple_of(t * rows, rows), rows)] + chosen(a, HALF - 1, t, 1)
            zo_st[a, t] = total.astype(BF).reshape(RL, PT, 128)
            if o:
                o_copy(a, t).start()
        zo_in[a, z] = zo_st[a, z]

    most = pl.ds(0, ZN - 1)
    remote(gin_z.at[most], gin_z.at[most], g_send, g_recv, blk, z).wait_recv()
    for col in range(4):
        total = gin_z[0, col].astype(F32)
        for s in range(1, ZN):
            total += gin_z[s, col].astype(F32)
        gsum[col] = total
    there = gsum.at[pl.ds(2 * (1 - up), 2)]
    q_copy = remote(there, gpart, p_send.at[3], p_recv.at[3], partner, z)
    q_copy.start()

    for a, ref in enumerate((out_ref, gin_ref)):
        remote(zo_in.at[a, most], zo_in.at[a, most], o_send.at[a], o_recv.at[a], blk, z).wait_recv()
        for s in range(ZN):
            for i in range(RL):
                ref[s * PT:(s + 1) * PT, i * 128:(i + 1) * 128] = zo_in[a, s, i]

    q_copy.wait_recv()
    for cl in range(2):
        own = gsum[2 * up + cl] + gpart[cl]
        for s in range(2):
            live = s < cnt_ref[cl]
            for ref, k in ((gup_ref, 0), (gdn_ref, 1)):
                ref[cl, s] = jnp.where(live, own[k, s], 0.0).astype(BF)

    for o in range(1, XC):
        row_a(o).wait_send()
    for o in range(1, YN):
        row_b(o).wait_send()
    for copy in (*w_copies, m_copy, q_copy):
        copy.wait_send()
    sent = pl.ds(0, ND - 1)
    for a in range(2):
        for buf, sem in (
            (zst.at[a, most], z_send), (zo_st.at[a, most], o_send),
            (tile_st.at[a, sent], d_send), (term_st.at[a, sent], t_send),
        ):
            remote(buf, buf, sem.at[a], sem.at[a], blk, z).wait_send()
    remote(gst.at[most], gst.at[most], g_send, g_recv, blk, z).wait_send()
    for k in range(2):
        remote(seven(k), seven(k), v_send.at[k], v_recv.at[k], blk, z).wait_send()


def place(*refs):
    for src, dst in zip(refs[:4], refs[4:]):
        dst[...] = src[...]


def per_device(inputs, grad_out, w_up, w_down, up_rows, slot_counts, keep_mask):
    tok, width = inputs.shape
    zn = lax.axis_size("tp")
    blocks = lax.axis_size("blk")
    xn = X_CHIPS
    yn = blocks // (2 * xn)
    pt, rl = tok // zn, width // 128
    half, xcn = yn // 2, 2 * xn
    nd, gt = half * xcn, xcn * pt
    rows = 128 // zn
    dims = (yn, xn, zn, pt, rl)
    vmem, smem = pl.BlockSpec(memory_space=pltpu.VMEM), pl.BlockSpec(memory_space=pltpu.SMEM)
    V, S = pltpu.VMEM, pltpu.SemaphoreType.DMA
    scratch = [
        V(inputs.shape, BF), V(inputs.shape, BF), V(w_up.shape, BF), V(w_down.shape, BF),
        V(keep_mask.shape[::-1], I32),
        V((2, zn, rl, pt, 128), BF),
        V((zn * rl, pt, 128), BF),
        V((zn * rl, pt, 128), BF),
        V((xcn, 8, 128), I32),
        V((yn, 8, 128), I32),
        pltpu.SMEM((yn, 8, 128), I32),
        V((4, 256, 128), BF),
        V((4, 128, 256), BF),
        V((yn, 16, gt), I32),
        V((2, half, 16, gt), I32),
        V((half, 16, gt), I32),
        V((2, half * gt, 256), F32),
        V((2, nd, 8, pt, 128), BF),
        V((2, nd, 8, pt, 128), BF),
        V((4, half * gt, 128), F32),
        V((4, half * gt, 128), BF),
        V((4, half * gt, 128), BF),
        V((2, nd, 8, pt, 128), BF),
        V((2, nd, 8, pt, 128), BF),
        V((nd, 8, 128), I32),
        V((zn * rl * pt, nd * 128), BF),
        V((zn * rl * pt, 128), F32),
        V((2, zn, rl, pt, 128), BF),
        V((2, zn, rl, pt, 128), BF),
        V((zn, 4, 2, 2, rows, 128), BF),
        V((zn, 4, 2, 2, rows, 128), BF),
        V((4, 2, 2, rows, 128), F32),
        V((2, 2, 2, rows, 128), F32),
        S((2,)), S((2,)), S((xcn,)), S((xcn,)), S((yn,)), S((yn,)), S((4,)), S((4,)),
        S((2,)), S((2, half)), S((2,)), S((2, half)), S((2,)), S((2,)), S, S, S, S((5,)), S((2,)), S((2,)),
    ]
    shape = jax.ShapeDtypeStruct
    shapes = (
        shape(inputs.shape, BF), shape(inputs.shape, BF),
        shape((2, 2, rows, 128), BF), shape((2, 2, rows, 128), BF),
    )
    results = pl.pallas_call(
        functools.partial(kernel, dims),
        out_shape=tuple(pltpu.VMEM(one.shape, one.dtype) for one in shapes),
        in_specs=[pl.BlockSpec(memory_space=pl.ANY)] * 5 + [smem] * 2,
        out_specs=(vmem,) * 4,
        scratch_shapes=scratch,
        compiler_params=pltpu.CompilerParams(
            collective_id=0, has_side_effects=True, vmem_limit_bytes=56 * 1024 * 1024
        ),
        cost_estimate=pl.CostEstimate(flops=10**10, bytes_accessed=10**7, transcendentals=10**6),
    )(inputs, grad_out, w_up, w_down, keep_mask.T, up_rows, slot_counts)
    results = [pltpu.with_memory_space_constraint(one, pltpu.VMEM) for one in results]
    return pl.pallas_call(place, out_shape=shapes, in_specs=[vmem] * 4, out_specs=(vmem,) * 4)(*results)


def solution(mesh):
    return jax.shard_map(
        per_device,
        mesh=mesh,
        in_specs=(
            P("blk", "tp"),
            P("blk", "tp"),
            P("blk", None, None, None),
            P("blk", None, None, None),
            P("blk", None),
            P("blk"),
            P(None, "blk"),
        ),
        out_specs=(
            P("blk", "tp"),
            P("blk", "tp"),
            P("blk", None, "tp", None),
            P("blk", None, "tp", None),
        ),
        check_vma=False,
    )
```

```python
import functools

import jax
import jax.numpy as jnp
from jax import lax
from jax.experimental import pallas as pl
from jax.experimental.pallas import tpu as pltpu
from jax.sharding import PartitionSpec as P

INV_ROOT_TWO = 0.7071067811865476
INV_ROOT_TAU = 0.3989422804014327
KEEP_SCALE = 1.25
MESH = pl.DeviceIdType.MESH
X_CHIPS = 4
BF = jnp.bfloat16
F32 = jnp.float32
I32 = jnp.int32


def dot(a, b, ca, cb):
    return lax.dot_general(a, b, (((ca,), (cb,)), ((), ())), preferred_element_type=F32)


def iota(shape, dim):
    return lax.broadcasted_iota(I32, shape, dim)


def hop(value, step, count):
    there = value + step
    there = jnp.where(there >= count, there - count, there)
    return jnp.where(there < 0, there + count, there)


def split(value, count):
    shift = count.bit_length() - 1
    assert count == 1 << shift
    return jnp.right_shift(value, shift), jnp.bitwise_and(value, count - 1)


def kernel(
    dims,
    x_hbm, dy_hbm, wu_hbm, wd_hbm, keep_hbm, rows_ref, cnt_ref,
    out_ref, gin_ref, gup_ref, gdn_ref,
    x_ref, dy_ref, wu_ref, wd_ref, keep_ref, zst, full_x, full_dy, rows_a, rows_b, rows_s, wu, wd, tokw, maskw, mask_st, scale,
    tile_st, tile_in, slope, hid, gpre, term_st, term_in, lanes, hot,
    acc, zo_st, zo_in, gst, gin_z, gsum, gpart,
    z_send, z_recv, a_send, a_recv, b_send, b_recv, p_send, p_recv,
    d_send, d_recv, t_send, t_recv, o_send, o_recv, g_send, g_recv, l_sem, in_sem, v_send, v_recv,
):
    YN, XN, ZN, PT, RL = dims
    XC = XN * 2
    HALF = YN // 2
    LO = HALF // 2 - 1
    ND = HALF * XC
    RB = RL * ZN
    GT = XC * PT
    blk, z = lax.axis_index("blk"), lax.axis_index("tp")
    c = lax.rem(blk, 2)
    x = lax.rem(blk // 2, XN)
    y = blk // XC
    xc = x * 2 + c
    up = jnp.where(y >= HALF, 1, 0)
    partner = hop(y, HALF, YN) * XC + xc

    def remote(src, dst, ss, rs, b, t):
        return pltpu.make_async_remote_copy(
            src_ref=src, dst_ref=dst, send_sem=ss, recv_sem=rs, device_id=(b, t), device_id_type=MESH
        )

    fetch = [
        pltpu.make_async_copy(src, dst, in_sem.at[k])
        for k, (src, dst) in enumerate(
            ((x_hbm, x_ref), (dy_hbm, dy_ref), (wu_hbm, wu_ref), (wd_hbm, wd_ref), (keep_hbm, keep_ref))
        )
    ]
    for one in fetch:
        one.start()

    order = [o for k in range(1, ZN // 2 + 1) for o in dict.fromkeys((k, ZN - k))]
    barrier = pltpu.get_barrier_semaphore()
    peers = []
    for zo in order:
        peers.append((blk, hop(z, zo, ZN)))
    for o in range(1, XC):
        peers.append((y * XC + hop(xc, o, XC), z))
    for o in range(1, YN):
        peers.append((hop(y, o, YN) * XC + xc, z))
    for b, t in peers:
        pl.semaphore_signal(barrier, inc=1, device_id=(b, t), device_id_type=MESH)

    full = (full_x, full_dy)
    lane = iota((8, 128), 1)
    mine = jnp.where(lane == 0, rows_ref[0, 0], jnp.where(lane == 1, rows_ref[0, 1],
                     jnp.where(lane == 2, rows_ref[1, 0], rows_ref[1, 1])))
    rows_a[xc] = mine
    for a, ref in enumerate((x_ref, dy_ref)):
        fetch[a].wait()
        for t in range(ZN):
            for i in range(RL):
                zst[a, t, i] = ref[t * PT:(t + 1) * PT, i * 128:(i + 1) * 128]
        full[a][pl.ds(z * RL, RL)] = zst[a, z]
    fetch[2].wait()
    fetch[3].wait()
    for cl in range(2):
        for s in range(2):
            live = s < cnt_ref[cl]
            wu[2 * up + cl, s * 128:(s + 1) * 128, :] = jnp.where(live, wu_ref[cl, s], jnp.zeros((), BF))
            wd[2 * up + cl, :, s * 128:(s + 1) * 128] = jnp.where(live, wd_ref[cl, s], jnp.zeros((), BF))
    pl.semaphore_wait(barrier, len(peers))

    def row_a(o):
        q = hop(xc, o, XC)
        return remote(rows_a.at[xc], rows_a.at[xc], a_send.at[o], a_recv.at[xc], y * XC + q, z)

    for o in range(1, XC):
        row_a(o).start()


    def z_copy(a, o):
        t = hop(z, o, ZN)
        return remote(zst.at[a, t], full[a].at[pl.ds(z * RL, RL)], z_send.at[a], z_recv.at[a], blk, t)

    for o in order:
        z_copy(0, o).start()

    def w_slice(k, half, at):
        rows = (256, 128)[k] // ZN
        return (wu, wd)[k].at[pl.ds(2 * half, 2), pl.ds(pl.multiple_of(at * rows, rows), rows)]

    w_copies = [
        remote(w_slice(k, up, z), w_slice(k, up, z), p_send.at[k], p_recv.at[k], partner, z) for k in range(2)
    ]
    for w_copy in w_copies:
        w_copy.start()

    def wait_a(o):
        q = hop(xc, o, XC)
        remote(rows_a.at[q], rows_a.at[q], a_send.at[o], a_recv.at[q], blk, z).wait_recv()

    for o in range(1, XC):
        wait_a(o)
    sub = iota((8, 128), 0)
    packed = rows_a[0]
    for q in range(1, XC):
        packed = jnp.where(sub == q, rows_a[q], packed)
    rows_b[y] = packed

    def row_b(o):
        q = hop(y, o, YN)
        return remote(rows_b.at[y], rows_b.at[y], b_send.at[o], b_recv.at[y], q * XC + xc, z)

    for o in range(1, YN):
        row_b(o).start()
    for o in range(1, YN):
        q = hop(y, o, YN)
        remote(rows_b.at[q], rows_b.at[q], b_send.at[o], b_recv.at[q], blk, z).wait_recv()
    to_scalar = pltpu.make_async_copy(rows_b, rows_s, l_sem)
    to_scalar.start()
    to_scalar.wait()

    x_order = [xo for xo in (2, 1, 0, 3) if xo < XN]

    def token_side(j, xo, co):
        xd, cd = hop(x, xo, XN), hop(c, co, 2)
        yd = hop(y, LO - j + cd, YN)
        return j * XC + xd * 2 + cd, yd, xd * 2 + cd, j * XC + xc

    def owner_side(j, xo, co):
        xd, cd = hop(x, xo, XN), hop(c, co, 2)
        yd = hop(y, j - LO - c, YN)
        return j * XC + xd * 2 + cd, yd, xd * 2 + cd, j * XC + xc

    def send_to(side, st, into, sends, recvs, a, j, xo, co):
        d, yd, xcd, at = side(j, xo, co)
        own = j == LO + c

        def near():
            pltpu.make_async_copy(st.at[a, d], into.at[a, at], recvs.at[a, j]).start()

        def far():
            remote(st.at[a, d], into.at[a, at], sends.at[a], recvs.at[a, j], yd * XC + xcd, z).start()

        if co == 0 and xo == 0:
            pl.when(own)(near)
            pl.when(jnp.logical_not(own))(far)
        else:
            far()

    def slot_rows(yd, xcd):
        low = jnp.where(yd >= HALF, yd - HALF, yd)
        return [rows_s[low + HALF * (k // 4), xcd, k % 4] for k in range(8)]

    def wait_z(a):
        others = full[a].at[pl.ds(0, (ZN - 1) * RL)]
        remote(others, others, z_send.at[a], z_recv.at[a], blk, z).wait_recv()

    def dispatch(a):
        @pl.loop(0, HALF)
        def _(j):
            for co in range(2):
                for xo in x_order:
                    d, yd, xcd, at = token_side(j, xo, co)
                    for k, row in enumerate(slot_rows(yd, xcd)):
                        tile_st[a, d, k] = full[a][row]
                    send_to(token_side, tile_st, tile_in, d_send, d_recv, a, j, xo, co)

    wait_z(0)
    for o in order:
        z_copy(1, o).start()
    for k in range(2):
        mine = w_slice(k, 1 - up, z)
        remote(mine, mine, p_send.at[k], p_recv.at[k], partner, z).wait_recv()
        for o in order:
            remote(mine, mine, v_send.at[k], v_recv.at[k], blk, hop(z, o, ZN)).start()
    dispatch(0)

    span = XC * ZN * PT
    r, l = iota((span, GT), 0), iota((span, GT), 1)
    share = ZN * PT
    (r, rest), (l, near) = split(r, share), split(l, PT)
    pick = jnp.where((r == l) & (rest == z * PT + near), 1.0, 0.0).astype(BF)
    fetch[4].wait()
    for g in range(YN):
        words = keep_ref[:, g * span:(g + 1) * span]
        low = jnp.bitwise_and(words, 255).astype(F32).astype(BF)
        high = jnp.right_shift(words, 8).astype(F32).astype(BF)
        found = dot(jnp.concatenate([low, high], axis=0), pick, 1, 0).astype(I32)
        tokw[g] = found[:16] + found[16:] * 256
    for j in range(HALF):
        maskw[up, j] = tokw[hop(y, j - LO - c, YN)]
        mask_st[j] = tokw[hop(hop(y, HALF, YN), j - LO - c, YN)]
    m_copy = remote(mask_st, maskw.at[up], p_send.at[2], p_recv.at[2], partner, z)
    m_copy.start()

    wait_z(1)
    dispatch(1)

    piece, near_token = split(lane, PT)

    @pl.loop(0, XN)
    def _(xo):
        for co in range(2):
            for j in range(HALF):
                d, yd, xcd, at = token_side(j, xo, co)
                value = near_token
                for k, row in enumerate(slot_rows(yd, xcd)):
                    value = jnp.where(piece == k, row * PT + near_token, value)
                lanes[d] = value

    @pl.loop(0, ND)
    def _(d):
        want = lanes[d][0:1, :]
        at = pl.ds(pl.multiple_of(d * 128, 128), 128)
        hot[:, at] = jnp.where(iota((RB * PT, 128), 0) == want, 1.0, 0.0).astype(BF)

    m_wait = remote(mask_st, maskw.at[1 - up], p_send.at[2], p_recv.at[2], partner, z)
    m_wait.wait_recv()
    er, el = iota((32, 256), 0), iota((32, 256), 1)
    (word, bit), (_, which) = split(el, 16), split(er, 16)
    spread = jnp.where((word == which) & ((bit >= 8) == (er >= 16)), 1.0, 0.0).astype(BF)
    shift = split(iota((GT, 256), 1), 8)[1]
    for h in range(2):
        for j in range(HALF):
            words = maskw[h, j]
            low = jnp.bitwise_and(words, 255).astype(F32).astype(BF)
            high = jnp.right_shift(words, 8).astype(F32).astype(BF)
            found = dot(jnp.concatenate([low, high], axis=0), spread, 0, 0).astype(I32)
            keep = jnp.bitwise_and(jnp.right_shift(found, shift), 1)
            scale[h, j * GT:(j + 1) * GT, :] = keep.astype(F32) * KEEP_SCALE
    def seven(k):
        rows = (256, 128)[k] // ZN
        return (wu, wd)[k].at[pl.ds(0, 2), pl.ds(0, (ZN - 1) * rows)]

    for k in range(2):
        remote(seven(k), seven(k), v_send.at[k], v_recv.at[k], blk, z).wait_recv()

    def wide(a, col, start, count):
        parts = [tile_in[a, pl.ds(start, count), 2 * col + s].reshape(count * PT, 128) for s in range(2)]
        return jnp.concatenate(parts, axis=1)

    def wait_group(buf, sem, a, g):
        block = buf.at[a, pl.ds(g * XC, XC)]
        remote(block, block, sem.at[a, g], sem.at[a, g], blk, z).wait_recv()

    def put(a, col, g, value):
        value = value.astype(BF)
        for s in range(2):
            term_st[a, pl.ds(g * XC, XC), 2 * col + s] = value[:, s * 128:(s + 1) * 128].reshape(XC, PT, 128)

    def send_group(a, g):
        for co in range(2):
            for xo in x_order:
                send_to(owner_side, term_st, term_in, t_send, t_recv, a, g, xo, co)

    @pl.loop(0, HALF)
    def _(g):
        wait_group(tile_in, d_recv, 0, g)
        toks = pl.ds(pl.multiple_of(g * GT, GT), GT)
        for col in range(4):
            pre = dot(wide(0, col, g * XC, XC), wu[col], 1, 0)
            part = 0.5 * (1.0 + lax.erf(pre * INV_ROOT_TWO))
            keep = scale[col // 2, toks, (col % 2) * 128:(col % 2 + 1) * 128]
            hidden = (pre * part * keep).astype(BF)
            slope[col, toks] = (part + pre * jnp.exp(-0.5 * pre * pre) * INV_ROOT_TAU) * keep
            hid[col, toks] = hidden
            put(0, col, g, dot(hidden, wd[col], 1, 0))
        send_group(0, g)

    @pl.loop(0, HALF)
    def _(g):
        wait_group(tile_in, d_recv, 1, g)
        toks = pl.ds(pl.multiple_of(g * GT, GT), GT)
        for col in range(4):
            grad = dot(wide(1, col, g * XC, XC), wd[col], 1, 1)
            grad = (grad * slope[col, toks]).astype(BF)
            gpre[col, toks] = grad
            put(1, col, g, dot(grad, wu[col], 1, 1))
        send_group(1, g)

    @pl.loop(0, 4)
    def _(col):
        grad_up = dot(wide(0, col, 0, ND), gpre[col], 0, 0).astype(BF)
        grad_dn = dot(hid[col], wide(1, col, 0, ND), 0, 0).astype(BF)
        rows = 128 // ZN
        for t in range(ZN):
            for s in range(2):
                gst[t, col, 0, s] = grad_up[s * 128 + t * rows:s * 128 + (t + 1) * rows, :]
                gst[t, col, 1, s] = grad_dn[t * rows:(t + 1) * rows, s * 128:(s + 1) * 128]

    def g_copy(o):
        t = hop(z, o, ZN)
        return remote(gst.at[t], gin_z.at[z], g_send, g_recv, blk, t)

    for o in order:
        g_copy(o).start()
    gin_z[z] = gst[z]

    def o_copy(a, t):
        return remote(zo_st.at[a, t], zo_in.at[a, z], o_send.at[a], o_recv.at[a], blk, t)

    rows = RL * PT
    deep = XC * 128

    def chosen(a, g, t, count):
        left = hot[pl.ds(pl.multiple_of(t * rows, rows), count * rows), pl.ds(pl.multiple_of(g * deep, deep), deep)]
        return dot(left, term_in[a, pl.ds(g * XC, XC)].reshape(deep, 128), 1, 0)

    for a in range(2):
        wait_group(term_in, t_recv, a, 0)

        @pl.loop(0, ZN // 2)
        def _(m):
            acc[pl.ds(pl.multiple_of(m * 2 * rows, rows), 2 * rows)] = chosen(a, 0, 2 * m, 2)

        @pl.loop(1, HALF - 1)
        def _(g):
            wait_group(term_in, t_recv, a, g)

            @pl.loop(0, ZN // 2)
            def _(m):
                acc[pl.ds(pl.multiple_of(m * 2 * rows, rows), 2 * rows)] += chosen(a, g, 2 * m, 2)

        wait_group(term_in, t_recv, a, HALF - 1)
        for o in (*order, 0):
            t = hop(z, o, ZN)
            total = acc[pl.ds(pl.multiple_of(t * rows, rows), rows)] + chosen(a, HALF - 1, t, 1)
            zo_st[a, t] = total.astype(BF).reshape(RL, PT, 128)
            if o:
                o_copy(a, t).start()
        zo_in[a, z] = zo_st[a, z]

    most = pl.ds(0, ZN - 1)
    remote(gin_z.at[most], gin_z.at[most], g_send, g_recv, blk, z).wait_recv()
    for col in range(4):
        total = gin_z[0, col].astype(F32)
        for s in range(1, ZN):
            total += gin_z[s, col].astype(F32)
        gsum[col] = total
    there = gsum.at[pl.ds(2 * (1 - up), 2)]
    q_copy = remote(there, gpart, p_send.at[3], p_recv.at[3], partner, z)
    q_copy.start()

    for a, ref in enumerate((out_ref, gin_ref)):
        remote(zo_in.at[a, most], zo_in.at[a, most], o_send.at[a], o_recv.at[a], blk, z).wait_recv()
        for s in range(ZN):
            for i in range(RL):
                ref[s * PT:(s + 1) * PT, i * 128:(i + 1) * 128] = zo_in[a, s, i]

    q_copy.wait_recv()
    for cl in range(2):
        own = gsum[2 * up + cl] + gpart[cl]
        for s in range(2):
            live = s < cnt_ref[cl]
            for ref, k in ((gup_ref, 0), (gdn_ref, 1)):
                ref[cl, s] = jnp.where(live, own[k, s], 0.0).astype(BF)

    for o in range(1, XC):
        row_a(o).wait_send()
    for o in range(1, YN):
        row_b(o).wait_send()
    for copy in (*w_copies, m_copy, q_copy):
        copy.wait_send()
    sent = pl.ds(0, ND - 1)
    for a in range(2):
        for buf, sem in (
            (zst.at[a, most], z_send), (zo_st.at[a, most], o_send),
            (tile_st.at[a, sent], d_send), (term_st.at[a, sent], t_send),
        ):
            remote(buf, buf, sem.at[a], sem.at[a], blk, z).wait_send()
    remote(gst.at[most], gst.at[most], g_send, g_recv, blk, z).wait_send()
    for k in range(2):
        remote(seven(k), seven(k), v_send.at[k], v_recv.at[k], blk, z).wait_send()


def place(*refs):
    for src, dst in zip(refs[:4], refs[4:]):
        dst[...] = src[...]


def per_device(inputs, grad_out, w_up, w_down, up_rows, slot_counts, keep_mask):
    tok, width = inputs.shape
    zn = lax.axis_size("tp")
    blocks = lax.axis_size("blk")
    xn = X_CHIPS
    yn = blocks // (2 * xn)
    pt, rl = tok // zn, width // 128
    half, xcn = yn // 2, 2 * xn
    nd, gt = half * xcn, xcn * pt
    rows = 128 // zn
    dims = (yn, xn, zn, pt, rl)
    vmem, smem = pl.BlockSpec(memory_space=pltpu.VMEM), pl.BlockSpec(memory_space=pltpu.SMEM)
    V, S = pltpu.VMEM, pltpu.SemaphoreType.DMA
    scratch = [
        V(inputs.shape, BF), V(inputs.shape, BF), V(w_up.shape, BF), V(w_down.shape, BF),
        V(keep_mask.shape[::-1], I32),
        V((2, zn, rl, pt, 128), BF),
        V((zn * rl, pt, 128), BF),
        V((zn * rl, pt, 128), BF),
        V((xcn, 8, 128), I32),
        V((yn, 8, 128), I32),
        pltpu.SMEM((yn, 8, 128), I32),
        V((4, 256, 128), BF),
        V((4, 128, 256), BF),
        V((yn, 16, gt), I32),
        V((2, half, 16, gt), I32),
        V((half, 16, gt), I32),
        V((2, half * gt, 256), F32),
        V((2, nd, 8, pt, 128), BF),
        V((2, nd, 8, pt, 128), BF),
        V((4, half * gt, 128), F32),
        V((4, half * gt, 128), BF),
        V((4, half * gt, 128), BF),
        V((2, nd, 8, pt, 128), BF),
        V((2, nd, 8, pt, 128), BF),
        V((nd, 8, 128), I32),
        V((zn * rl * pt, nd * 128), BF),
        V((zn * rl * pt, 128), F32),
        V((2, zn, rl, pt, 128), BF),
        V((2, zn, rl, pt, 128), BF),
        V((zn, 4, 2, 2, rows, 128), BF),
        V((zn, 4, 2, 2, rows, 128), BF),
        V((4, 2, 2, rows, 128), F32),
        V((2, 2, 2, rows, 128), F32),
        S((2,)), S((2,)), S((xcn,)), S((xcn,)), S((yn,)), S((yn,)), S((4,)), S((4,)),
        S((2,)), S((2, half)), S((2,)), S((2, half)), S((2,)), S((2,)), S, S, S, S((5,)), S((2,)), S((2,)),
    ]
    shape = jax.ShapeDtypeStruct
    shapes = (
        shape(inputs.shape, BF), shape(inputs.shape, BF),
        shape((2, 2, rows, 128), BF), shape((2, 2, rows, 128), BF),
    )
    results = pl.pallas_call(
        functools.partial(kernel, dims),
        out_shape=tuple(pltpu.VMEM(one.shape, one.dtype) for one in shapes),
        in_specs=[pl.BlockSpec(memory_space=pl.ANY)] * 5 + [smem] * 2,
        out_specs=(vmem,) * 4,
        scratch_shapes=scratch,
        compiler_params=pltpu.CompilerParams(
            collective_id=0, has_side_effects=True, vmem_limit_bytes=56 * 1024 * 1024
        ),
        cost_estimate=pl.CostEstimate(flops=10**10, bytes_accessed=10**7, transcendentals=10**6),
    )(inputs, grad_out, w_up, w_down, keep_mask.T, up_rows, slot_counts)
    results = [pltpu.with_memory_space_constraint(one, pltpu.VMEM) for one in results]
    return pl.pallas_call(place, out_shape=shapes, in_specs=[vmem] * 4, out_specs=(vmem,) * 4)(*results)


def solution(mesh):
    return jax.shard_map(
        per_device,
        mesh=mesh,
        in_specs=(
            P("blk", "tp"),
            P("blk", "tp"),
            P("blk", None, None, None),
            P("blk", None, None, None),
            P("blk", None),
            P("blk"),
            P(None, "blk"),
        ),
        out_specs=(
            P("blk", "tp"),
            P("blk", "tp"),
            P("blk", None, "tp", None),
            P("blk", None, "tp", None),
        ),
        check_vma=False,
    )
```

```python
import functools

import jax
import jax.numpy as jnp
from jax import lax
from jax.experimental import pallas as pl
from jax.experimental.pallas import tpu as pltpu
from jax.sharding import PartitionSpec as P

INV_ROOT_TWO = 0.7071067811865476
INV_ROOT_TAU = 0.3989422804014327
KEEP_SCALE = 1.25
MESH = pl.DeviceIdType.MESH
X_CHIPS = 4
BF = jnp.bfloat16
F32 = jnp.float32
I32 = jnp.int32


def dot(a, b, ca, cb):
    return lax.dot_general(a, b, (((ca,), (cb,)), ((), ())), preferred_element_type=F32)


def iota(shape, dim):
    return lax.broadcasted_iota(I32, shape, dim)


def hop(value, step, count):
    there = value + step
    there = jnp.where(there >= count, there - count, there)
    return jnp.where(there < 0, there + count, there)


def split(value, count):
    shift = count.bit_length() - 1
    assert count == 1 << shift
    return jnp.right_shift(value, shift), jnp.bitwise_and(value, count - 1)


def kernel(
    dims,
    x_hbm, dy_hbm, wu_hbm, wd_hbm, keep_hbm, rows_ref, cnt_ref,
    out_ref, gin_ref, gup_ref, gdn_ref,
    x_ref, dy_ref, wu_ref, wd_ref, keep_ref, zst, full_x, full_dy, rows_a, rows_b, rows_s, wu, wd, tokw, maskw, mask_st, scale,
    tile_st, tile_in, slope, hid, gpre, term_st, term_in, lanes, hot,
    acc, zo_st, zo_in, gst, gin_z, gsum, gpart,
    z_send, z_recv, a_send, a_recv, b_send, b_recv, p_send, p_recv,
    d_send, d_recv, t_send, t_recv, o_send, o_recv, g_send, g_recv, l_sem, in_sem, v_send, v_recv,
):
    YN, XN, ZN, PT, RL = dims
    XC = XN * 2
    HALF = YN // 2
    LO = HALF // 2 - 1
    ND = HALF * XC
    RB = RL * ZN
    GT = XC * PT
    blk, z = lax.axis_index("blk"), lax.axis_index("tp")
    c = lax.rem(blk, 2)
    x = lax.rem(blk // 2, XN)
    y = blk // XC
    xc = x * 2 + c
    up = jnp.where(y >= HALF, 1, 0)
    partner = hop(y, HALF, YN) * XC + xc

    def remote(src, dst, ss, rs, b, t):
        return pltpu.make_async_remote_copy(
            src_ref=src, dst_ref=dst, send_sem=ss, recv_sem=rs, device_id=(b, t), device_id_type=MESH
        )

    fetch = [
        pltpu.make_async_copy(src, dst, in_sem.at[k])
        for k, (src, dst) in enumerate(
            ((x_hbm, x_ref), (dy_hbm, dy_ref), (wu_hbm, wu_ref), (wd_hbm, wd_ref), (keep_hbm, keep_ref))
        )
    ]
    fetch[0].start()

    order = [o for k in range(1, ZN // 2 + 1) for o in dict.fromkeys((k, ZN - k))]
    barrier = pltpu.get_barrier_semaphore()
    peers = []
    for zo in order:
        peers.append((blk, hop(z, zo, ZN)))
    for o in range(1, XC):
        peers.append((y * XC + hop(xc, o, XC), z))
    for o in range(1, YN):
        peers.append((hop(y, o, YN) * XC + xc, z))
    for b, t in peers:
        pl.semaphore_signal(barrier, inc=1, device_id=(b, t), device_id_type=MESH)
    for one in fetch[1:]:
        one.start()

    full = (full_x, full_dy)
    lane = iota((8, 128), 1)
    mine = jnp.where(lane == 0, rows_ref[0, 0], jnp.where(lane == 1, rows_ref[0, 1],
                     jnp.where(lane == 2, rows_ref[1, 0], rows_ref[1, 1])))
    rows_a[xc] = mine

    def stage(a, ref):
        fetch[a].wait()
        for t in range(ZN):
            for i in range(RL):
                zst[a, t, i] = ref[t * PT:(t + 1) * PT, i * 128:(i + 1) * 128]
        full[a][pl.ds(z * RL, RL)] = zst[a, z]

    stage(0, x_ref)
    pl.semaphore_wait(barrier, len(peers))

    def row_a(o):
        q = hop(xc, o, XC)
        return remote(rows_a.at[xc], rows_a.at[xc], a_send.at[o], a_recv.at[xc], y * XC + q, z)

    def z_copy(a, o):
        t = hop(z, o, ZN)
        return remote(zst.at[a, t], full[a].at[pl.ds(z * RL, RL)], z_send.at[a], z_recv.at[a], blk, t)

    for o in order:
        z_copy(0, o).start()
    for o in range(1, XC):
        row_a(o).start()
    stage(1, dy_ref)
    fetch[2].wait()
    fetch[3].wait()
    for cl in range(2):
        for s in range(2):
            live = s < cnt_ref[cl]
            wu[2 * up + cl, s * 128:(s + 1) * 128, :] = jnp.where(live, wu_ref[cl, s], jnp.zeros((), BF))
            wd[2 * up + cl, :, s * 128:(s + 1) * 128] = jnp.where(live, wd_ref[cl, s], jnp.zeros((), BF))

    def w_slice(k, half, at):
        rows = (256, 128)[k] // ZN
        return (wu, wd)[k].at[pl.ds(2 * half, 2), pl.ds(pl.multiple_of(at * rows, rows), rows)]

    w_copies = [
        remote(w_slice(k, up, z), w_slice(k, up, z), p_send.at[k], p_recv.at[k], partner, z) for k in range(2)
    ]
    for w_copy in w_copies:
        w_copy.start()

    def wait_a(o):
        q = hop(xc, o, XC)
        remote(rows_a.at[q], rows_a.at[q], a_send.at[o], a_recv.at[q], blk, z).wait_recv()

    for o in range(1, XC):
        wait_a(o)
    sub = iota((8, 128), 0)
    packed = rows_a[0]
    for q in range(1, XC):
        packed = jnp.where(sub == q, rows_a[q], packed)
    rows_b[y] = packed

    def row_b(o):
        q = hop(y, o, YN)
        return remote(rows_b.at[y], rows_b.at[y], b_send.at[o], b_recv.at[y], q * XC + xc, z)

    for o in range(1, YN):
        row_b(o).start()
    for o in range(1, YN):
        q = hop(y, o, YN)
        remote(rows_b.at[q], rows_b.at[q], b_send.at[o], b_recv.at[q], blk, z).wait_recv()
    to_scalar = pltpu.make_async_copy(rows_b, rows_s, l_sem)
    to_scalar.start()
    to_scalar.wait()

    x_order = [xo for xo in (2, 1, 0, 3) if xo < XN]

    def token_side(j, xo, co):
        xd, cd = hop(x, xo, XN), hop(c, co, 2)
        yd = hop(y, LO - j + cd, YN)
        return j * XC + xd * 2 + cd, yd, xd * 2 + cd, j * XC + xc

    def owner_side(j, xo, co):
        xd, cd = hop(x, xo, XN), hop(c, co, 2)
        yd = hop(y, j - LO - c, YN)
        return j * XC + xd * 2 + cd, yd, xd * 2 + cd, j * XC + xc

    def send_to(side, st, into, sends, recvs, a, j, xo, co):
        d, yd, xcd, at = side(j, xo, co)
        own = j == LO + c

        def near():
            pltpu.make_async_copy(st.at[a, d], into.at[a, at], recvs.at[a, j]).start()

        def far():
            remote(st.at[a, d], into.at[a, at], sends.at[a], recvs.at[a, j], yd * XC + xcd, z).start()

        if co == 0 and xo == 0:
            pl.when(own)(near)
            pl.when(jnp.logical_not(own))(far)
        else:
            far()

    def slot_rows(yd, xcd):
        low = jnp.where(yd >= HALF, yd - HALF, yd)
        return [rows_s[low + HALF * (k // 4), xcd, k % 4] for k in range(8)]

    def wait_z(a):
        others = full[a].at[pl.ds(0, (ZN - 1) * RL)]
        remote(others, others, z_send.at[a], z_recv.at[a], blk, z).wait_recv()

    def dispatch(a):
        @pl.loop(0, HALF)
        def _(j):
            for co in range(2):
                for xo in x_order:
                    d, yd, xcd, at = token_side(j, xo, co)
                    for k, row in enumerate(slot_rows(yd, xcd)):
                        tile_st[a, d, k] = full[a][row]
                    send_to(token_side, tile_st, tile_in, d_send, d_recv, a, j, xo, co)

    wait_z(0)
    for o in order:
        z_copy(1, o).start()
    for k in range(2):
        mine = w_slice(k, 1 - up, z)
        remote(mine, mine, p_send.at[k], p_recv.at[k], partner, z).wait_recv()
        for o in order:
            remote(mine, mine, v_send.at[k], v_recv.at[k], blk, hop(z, o, ZN)).start()
    dispatch(0)

    span = XC * ZN * PT
    r, l = iota((span, GT), 0), iota((span, GT), 1)
    share = ZN * PT
    (r, rest), (l, near) = split(r, share), split(l, PT)
    pick = jnp.where((r == l) & (rest == z * PT + near), 1.0, 0.0).astype(BF)
    fetch[4].wait()
    for g in range(YN):
        words = keep_ref[:, g * span:(g + 1) * span]
        low = jnp.bitwise_and(words, 255).astype(F32).astype(BF)
        high = jnp.right_shift(words, 8).astype(F32).astype(BF)
        found = dot(jnp.concatenate([low, high], axis=0), pick, 1, 0).astype(I32)
        tokw[g] = found[:16] + found[16:] * 256
    for j in range(HALF):
        maskw[up, j] = tokw[hop(y, j - LO - c, YN)]
        mask_st[j] = tokw[hop(hop(y, HALF, YN), j - LO - c, YN)]
    m_copy = remote(mask_st, maskw.at[up], p_send.at[2], p_recv.at[2], partner, z)
    m_copy.start()

    wait_z(1)
    dispatch(1)

    piece, near_token = split(lane, PT)

    @pl.loop(0, XN)
    def _(xo):
        for co in range(2):
            for j in range(HALF):
                d, yd, xcd, at = token_side(j, xo, co)
                value = near_token
                for k, row in enumerate(slot_rows(yd, xcd)):
                    value = jnp.where(piece == k, row * PT + near_token, value)
                lanes[d] = value

    @pl.loop(0, ND)
    def _(d):
        want = lanes[d][0:1, :]
        at = pl.ds(pl.multiple_of(d * 128, 128), 128)
        hot[:, at] = jnp.where(iota((RB * PT, 128), 0) == want, 1.0, 0.0).astype(BF)

    m_wait = remote(mask_st, maskw.at[1 - up], p_send.at[2], p_recv.at[2], partner, z)
    m_wait.wait_recv()
    er, el = iota((32, 256), 0), iota((32, 256), 1)
    (word, bit), (_, which) = split(el, 16), split(er, 16)
    spread = jnp.where((word == which) & ((bit >= 8) == (er >= 16)), 1.0, 0.0).astype(BF)
    shift = split(iota((GT, 256), 1), 8)[1]
    for h in range(2):
        for j in range(HALF):
            words = maskw[h, j]
            low = jnp.bitwise_and(words, 255).astype(F32).astype(BF)
            high = jnp.right_shift(words, 8).astype(F32).astype(BF)
            found = dot(jnp.concatenate([low, high], axis=0), spread, 0, 0).astype(I32)
            keep = jnp.bitwise_and(jnp.right_shift(found, shift), 1)
            scale[h, j * GT:(j + 1) * GT, :] = keep.astype(F32) * KEEP_SCALE
    def seven(k):
        rows = (256, 128)[k] // ZN
        return (wu, wd)[k].at[pl.ds(0, 2), pl.ds(0, (ZN - 1) * rows)]

    for k in range(2):
        remote(seven(k), seven(k), v_send.at[k], v_recv.at[k], blk, z).wait_recv()

    def wide(a, col, start, count):
        parts = [tile_in[a, pl.ds(start, count), 2 * col + s].reshape(count * PT, 128) for s in range(2)]
        return jnp.concatenate(parts, axis=1)

    def wait_group(buf, sem, a, g):
        block = buf.at[a, pl.ds(g * XC, XC)]
        remote(block, block, sem.at[a, g], sem.at[a, g], blk, z).wait_recv()

    def put(a, col, g, value):
        value = value.astype(BF)
        for s in range(2):
            term_st[a, pl.ds(g * XC, XC), 2 * col + s] = value[:, s * 128:(s + 1) * 128].reshape(XC, PT, 128)

    def send_group(a, g):
        for co in range(2):
            for xo in x_order:
                send_to(owner_side, term_st, term_in, t_send, t_recv, a, g, xo, co)

    @pl.loop(0, HALF)
    def _(g):
        wait_group(tile_in, d_recv, 0, g)
        toks = pl.ds(pl.multiple_of(g * GT, GT), GT)
        for col in range(4):
            pre = dot(wide(0, col, g * XC, XC), wu[col], 1, 0)
            part = 0.5 * (1.0 + lax.erf(pre * INV_ROOT_TWO))
            keep = scale[col // 2, toks, (col % 2) * 128:(col % 2 + 1) * 128]
            hidden = (pre * part * keep).astype(BF)
            slope[col, toks] = (part + pre * jnp.exp(-0.5 * pre * pre) * INV_ROOT_TAU) * keep
            hid[col, toks] = hidden
            put(0, col, g, dot(hidden, wd[col], 1, 0))
        send_group(0, g)

    @pl.loop(0, HALF)
    def _(g):
        wait_group(tile_in, d_recv, 1, g)
        toks = pl.ds(pl.multiple_of(g * GT, GT), GT)
        for col in range(4):
            grad = dot(wide(1, col, g * XC, XC), wd[col], 1, 1)
            grad = (grad * slope[col, toks]).astype(BF)
            gpre[col, toks] = grad
            put(1, col, g, dot(grad, wu[col], 1, 1))
        send_group(1, g)

    @pl.loop(0, 4)
    def _(col):
        grad_up = dot(wide(0, col, 0, ND), gpre[col], 0, 0).astype(BF)
        grad_dn = dot(hid[col], wide(1, col, 0, ND), 0, 0).astype(BF)
        rows = 128 // ZN
        for t in range(ZN):
            for s in range(2):
                gst[t, col, 0, s] = grad_up[s * 128 + t * rows:s * 128 + (t + 1) * rows, :]
                gst[t, col, 1, s] = grad_dn[t * rows:(t + 1) * rows, s * 128:(s + 1) * 128]

    def g_copy(o):
        t = hop(z, o, ZN)
        return remote(gst.at[t], gin_z.at[z], g_send, g_recv, blk, t)

    for o in order:
        g_copy(o).start()
    gin_z[z] = gst[z]

    def o_copy(a, t):
        return remote(zo_st.at[a, t], zo_in.at[a, z], o_send.at[a], o_recv.at[a], blk, t)

    rows = RL * PT
    deep = XC * 128

    def chosen(a, g, t, count):
        left = hot[pl.ds(pl.multiple_of(t * rows, rows), count * rows), pl.ds(pl.multiple_of(g * deep, deep), deep)]
        return dot(left, term_in[a, pl.ds(g * XC, XC)].reshape(deep, 128), 1, 0)

    for a in range(2):
        wait_group(term_in, t_recv, a, 0)

        @pl.loop(0, ZN // 2)
        def _(m):
            acc[pl.ds(pl.multiple_of(m * 2 * rows, rows), 2 * rows)] = chosen(a, 0, 2 * m, 2)

        @pl.loop(1, HALF - 1)
        def _(g):
            wait_group(term_in, t_recv, a, g)

            @pl.loop(0, ZN // 2)
            def _(m):
                acc[pl.ds(pl.multiple_of(m * 2 * rows, rows), 2 * rows)] += chosen(a, g, 2 * m, 2)

        wait_group(term_in, t_recv, a, HALF - 1)
        for o in (*order, 0):
            t = hop(z, o, ZN)
            total = acc[pl.ds(pl.multiple_of(t * rows, rows), rows)] + chosen(a, HALF - 1, t, 1)
            zo_st[a, t] = total.astype(BF).reshape(RL, PT, 128)
            if o:
                o_copy(a, t).start()
        zo_in[a, z] = zo_st[a, z]

    most = pl.ds(0, ZN - 1)
    remote(gin_z.at[most], gin_z.at[most], g_send, g_recv, blk, z).wait_recv()
    for col in range(4):
        total = gin_z[0, col].astype(F32)
        for s in range(1, ZN):
            total += gin_z[s, col].astype(F32)
        gsum[col] = total
    there = gsum.at[pl.ds(2 * (1 - up), 2)]
    q_copy = remote(there, gpart, p_send.at[3], p_recv.at[3], partner, z)
    q_copy.start()

    for a, ref in enumerate((out_ref, gin_ref)):
        remote(zo_in.at[a, most], zo_in.at[a, most], o_send.at[a], o_recv.at[a], blk, z).wait_recv()
        for s in range(ZN):
            for i in range(RL):
                ref[s * PT:(s + 1) * PT, i * 128:(i + 1) * 128] = zo_in[a, s, i]
        if a == 0:
            q_copy.wait_recv()
            for cl in range(2):
                own = gsum[2 * up + cl] + gpart[cl]
                for s in range(2):
                    live = s < cnt_ref[cl]
                    for ref, k in ((gup_ref, 0), (gdn_ref, 1)):
                        ref[cl, s] = jnp.where(live, own[k, s], 0.0).astype(BF)

    for o in range(1, XC):
        row_a(o).wait_send()
    for o in range(1, YN):
        row_b(o).wait_send()
    for copy in (*w_copies, m_copy, q_copy):
        copy.wait_send()
    sent = pl.ds(0, ND - 1)
    for a in range(2):
        for buf, sem in (
            (zst.at[a, most], z_send), (zo_st.at[a, most], o_send),
            (tile_st.at[a, sent], d_send), (term_st.at[a, sent], t_send),
        ):
            remote(buf, buf, sem.at[a], sem.at[a], blk, z).wait_send()
    remote(gst.at[most], gst.at[most], g_send, g_recv, blk, z).wait_send()
    for k in range(2):
        remote(seven(k), seven(k), v_send.at[k], v_recv.at[k], blk, z).wait_send()


def place(*refs):
    for src, dst in zip(refs[:4], refs[4:]):
        dst[...] = src[...]


def per_device(inputs, grad_out, w_up, w_down, up_rows, slot_counts, keep_mask):
    tok, width = inputs.shape
    zn = lax.axis_size("tp")
    blocks = lax.axis_size("blk")
    xn = X_CHIPS
    yn = blocks // (2 * xn)
    pt, rl = tok // zn, width // 128
    half, xcn = yn // 2, 2 * xn
    nd, gt = half * xcn, xcn * pt
    rows = 128 // zn
    dims = (yn, xn, zn, pt, rl)
    vmem, smem = pl.BlockSpec(memory_space=pltpu.VMEM), pl.BlockSpec(memory_space=pltpu.SMEM)
    V, S = pltpu.VMEM, pltpu.SemaphoreType.DMA
    scratch = [
        V(inputs.shape, BF), V(inputs.shape, BF), V(w_up.shape, BF), V(w_down.shape, BF),
        V(keep_mask.shape[::-1], I32),
        V((2, zn, rl, pt, 128), BF),
        V((zn * rl, pt, 128), BF),
        V((zn * rl, pt, 128), BF),
        V((xcn, 8, 128), I32),
        V((yn, 8, 128), I32),
        pltpu.SMEM((yn, 8, 128), I32),
        V((4, 256, 128), BF),
        V((4, 128, 256), BF),
        V((yn, 16, gt), I32),
        V((2, half, 16, gt), I32),
        V((half, 16, gt), I32),
        V((2, half * gt, 256), F32),
        V((2, nd, 8, pt, 128), BF),
        V((2, nd, 8, pt, 128), BF),
        V((4, half * gt, 128), F32),
        V((4, half * gt, 128), BF),
        V((4, half * gt, 128), BF),
        V((2, nd, 8, pt, 128), BF),
        V((2, nd, 8, pt, 128), BF),
        V((nd, 8, 128), I32),
        V((zn * rl * pt, nd * 128), BF),
        V((zn * rl * pt, 128), F32),
        V((2, zn, rl, pt, 128), BF),
        V((2, zn, rl, pt, 128), BF),
        V((zn, 4, 2, 2, rows, 128), BF),
        V((zn, 4, 2, 2, rows, 128), BF),
        V((4, 2, 2, rows, 128), F32),
        V((2, 2, 2, rows, 128), F32),
        S((2,)), S((2,)), S((xcn,)), S((xcn,)), S((yn,)), S((yn,)), S((4,)), S((4,)),
        S((2,)), S((2, half)), S((2,)), S((2, half)), S((2,)), S((2,)), S, S, S, S((5,)), S((2,)), S((2,)),
    ]
    shape = jax.ShapeDtypeStruct
    shapes = (
        shape(inputs.shape, BF), shape(inputs.shape, BF),
        shape((2, 2, rows, 128), BF), shape((2, 2, rows, 128), BF),
    )
    results = pl.pallas_call(
        functools.partial(kernel, dims),
        out_shape=tuple(pltpu.VMEM(one.shape, one.dtype) for one in shapes),
        in_specs=[pl.BlockSpec(memory_space=pl.ANY)] * 5 + [smem] * 2,
        out_specs=(vmem,) * 4,
        scratch_shapes=scratch,
        compiler_params=pltpu.CompilerParams(
            collective_id=0, has_side_effects=True, vmem_limit_bytes=56 * 1024 * 1024
        ),
        cost_estimate=pl.CostEstimate(flops=10**10, bytes_accessed=10**7, transcendentals=10**6),
    )(inputs, grad_out, w_up, w_down, keep_mask.T, up_rows, slot_counts)
    results = [pltpu.with_memory_space_constraint(one, pltpu.VMEM) for one in results]
    return pl.pallas_call(place, out_shape=shapes, in_specs=[vmem] * 4, out_specs=(vmem,) * 4)(*results)


def solution(mesh):
    return jax.shard_map(
        per_device,
        mesh=mesh,
        in_specs=(
            P("blk", "tp"),
            P("blk", "tp"),
            P("blk", None, None, None),
            P("blk", None, None, None),
            P("blk", None),
            P("blk"),
            P(None, "blk"),
        ),
        out_specs=(
            P("blk", "tp"),
            P("blk", "tp"),
            P("blk", None, "tp", None),
            P("blk", None, "tp", None),
        ),
        check_vma=False,
    )
```
